32 devices in a mesh: wide: 16 (over z, x, core), narrow: 2 (over y).
Axes of the slice: x: 2, y: 2, z: 4, core: 2. Of those that a mesh axis runs over, the one named last changes fastest.
Arguments:
- tokens: bfloat16 [16384, 768], P(('wide', 'narrow')), may hold values from -6 to 6
- segment_index_rows: int32 [32, 512], P(('wide', 'narrow')), may hold values from 0 to 3, never falling along the last dimension, each value on 1 to 256 neighbouring positions
- query_key_value_weight: bfloat16 [2, 768, 2304], P(None, None, ('wide', 'narrow')), may hold values from -0.21875 to 0.21875
- attention_output_weight: bfloat16 [2, 768, 768], P(None, None, ('wide', 'narrow')), may hold values from -0.625 to 0.625
- feedforward_up_weight: bfloat16 [2, 768, 3072], P(None, None, ('wide', 'narrow')), may hold values from -0.21875 to 0.21875
- feedforward_down_weight: bfloat16 [2, 3072, 768], P(None, ('wide', 'narrow')), may hold values from -0.109375 to 0.109375
- fixed_bias_stack: bfloat16 [2, 6144], P(None, ('wide', 'narrow')), may hold values from -1.5 to 1.5
- layer_norm_gains: bfloat16 [2, 2, 768], P(None, None, ('wide', 'narrow')), may hold values from 0.5 to 1.5
- layer_norm_shifts: bfloat16 [2, 2, 768], P(None, None, ('wide', 'narrow')), may hold values from -1.5 to 1.5
- adapter_down_factor: bfloat16 [2, 2, 768, 8], replicated, may hold values from -0.21875 to 0.21875
- adapter_up_factor: bfloat16 [2, 2, 8, 768], replicated, may hold values from -0.5 to 0.5
- output_gradient: bfloat16 [16384, 768], P(('wide', 'narrow')), may hold values from -6 to 6
Outputs:
- block_out: bfloat16 [16384, 768], P(('wide', 'narrow'))
- input_grad: bfloat16 [16384, 768], P(('wide', 'narrow'))
- grad_down: float32 [2, 2, 768, 8], P(None, None, 'narrow')
- grad_up: float32 [2, 2, 8, 768], P(None, None, None, 'narrow')
The draws below stay inside these ranges and needn't reach their ends.
Inputs may be any that keep to these rules, and one draw needn't show every extreme that they name: `segment_index_rows`: ids never fall along a pack; each of the 4 ids covers one run of rows of the pack.
All inputs are finite; a program needn't handle non-finite values.
Results may differ from the reference program's by a relative error of at most 0.024.
Values may be sent and summed in bfloat16 or wider, within the bound.
A program may use at most 256 MiB of HBM per device.

```python
import math
import jax
import jax.numpy as jnp
import numpy as np
from jax import lax

MODEL_DIMENSION = 768
HEADS = 12
FF = 3072
ADAPTER_RANK = 8
ENCODER_LAYERS = 2
SEQ = 512
SEGS = 4
PACKS = 32
TOKENS = 16384


def block_scale(key, extent, shards, least, top_value):
    loudness, own = 1.0, jax.random.fold_in(key, 6)
    for position, shards_of in shards:
        draws = jnp.exp(jax.random.uniform(jax.random.fold_in(own, position), (shards_of,), jnp.float32, least / len(shards), top_value / len(shards)))
        loudness = loudness * jnp.repeat(draws, extent[position] // shards_of).reshape([-1 if axis == position else 1 for axis in range(len(extent))])
    return loudness


def length_profile(count, total, most, slope):
    loads = [(1 << 20) // math.isqrt(rank ** slope) + 1 for rank in range(2, count + 1)]
    rest, counts = total - most - (count - 1), [1] * (count - 1)
    while rest > 0:
        candidates = [i for i in range(count - 1) if counts[i] < most]
        whole, left = sum([loads[i] for i in candidates]), rest
        for i in candidates:
            addition = min(most - counts[i], max(1, left * loads[i] // whole), rest)
            counts[i] = counts[i] + addition
            rest = rest - addition
    return np.array([most] + counts)


def uneven(key, count, total, reach, slope):
    if count == 2:
        one = jax.random.randint(key, (), max(1, total - reach), min(reach, total - 1) + 1)
        return jnp.stack([one, total - one])
    tallies = jnp.asarray(length_profile(count, total, reach, slope), jnp.int32)
    pairs = (count - 1) // 2
    donor, taker = tallies[1:1 + 2 * pairs:2], tallies[2:2 + 2 * pairs:2]
    margin = jnp.minimum(donor - 1, reach - taker)
    shifted = jax.random.randint(jax.random.fold_in(key, 1), (pairs,), 0, 1 << 20) % (margin + 1)
    tallies = tallies.at[1:1 + 2 * pairs:2].set(donor - shifted).at[2:2 + 2 * pairs:2].set(taker + shifted)
    return tallies[jax.random.permutation(jax.random.fold_in(key, 2), count)]


def gaussian(own_key, shape, scale, bound, pieces=(), dtype=jnp.bfloat16):
    gain = block_scale(own_key, shape, pieces, -0.22, 0.18) if pieces else 1.0
    values = jax.random.normal(own_key, shape, jnp.float32) * scale * gain
    return jnp.minimum(jnp.maximum(values, -bound), bound).astype(dtype)


def setup_inputs(seed: int = 0) -> dict:
    streams_of = jax.random.split(jax.random.key(seed), 13)
    tokens = gaussian(streams_of[0], (TOKENS, MODEL_DIMENSION), 1.0, 6.0, ((0, 32),))
    segment_index_rows = jax.vmap(lambda own: jnp.searchsorted(jnp.cumsum(uneven(own, SEGS, SEQ, SEQ // 2, 2)), jnp.arange(SEQ), side="right"))(jax.random.split(streams_of[1], PACKS)).reshape((PACKS, SEQ)).astype(jnp.int32)
    query_key_value_weight = gaussian(streams_of[2], (ENCODER_LAYERS, MODEL_DIMENSION, 3 * MODEL_DIMENSION), MODEL_DIMENSION ** -0.5, 0.21875, ((2, 32),))
    attention_output_weight = gaussian(streams_of[3], (ENCODER_LAYERS, MODEL_DIMENSION, MODEL_DIMENSION), (MODEL_DIMENSION // 8) ** -0.5, 0.625, ((2, 32),))
    feedforward_up_weight = gaussian(streams_of[4], (ENCODER_LAYERS, MODEL_DIMENSION, FF), MODEL_DIMENSION ** -0.5, 0.21875, ((2, 32),))
    feedforward_down_weight = gaussian(streams_of[5], (ENCODER_LAYERS, FF, MODEL_DIMENSION), FF ** -0.5, 0.109375, ((1, 32),))
    fixed_bias_stack = gaussian(streams_of[6], (ENCODER_LAYERS, 4 * MODEL_DIMENSION + FF), 0.3, 1.5, ((1, 32),))
    layer_norm_gains = jnp.clip(1.0 + 0.1 * jax.random.normal(streams_of[7], (ENCODER_LAYERS, 2, MODEL_DIMENSION), jnp.float32), 0.5, 1.5).astype(jnp.bfloat16)
    layer_norm_shifts = gaussian(streams_of[8], (ENCODER_LAYERS, 2, MODEL_DIMENSION), 0.3, 1.5, ((2, 32),))
    adapter_down_factor = gaussian(streams_of[9], (ENCODER_LAYERS, 2, MODEL_DIMENSION, ADAPTER_RANK), MODEL_DIMENSION ** -0.5, 0.21875)
    adapter_up_factor = gaussian(streams_of[10], (ENCODER_LAYERS, 2, ADAPTER_RANK, MODEL_DIMENSION), 0.1, 0.5)
    output_gradient = gaussian(streams_of[11], (TOKENS, MODEL_DIMENSION), 1.0, 6.0, ((0, 32),))
    return {"tokens": tokens, "segment_index_rows": segment_index_rows, "query_key_value_weight": query_key_value_weight, "attention_output_weight": attention_output_weight, "feedforward_up_weight": feedforward_up_weight, "feedforward_down_weight": feedforward_down_weight, "fixed_bias_stack": fixed_bias_stack, "layer_norm_gains": layer_norm_gains, "layer_norm_shifts": layer_norm_shifts, "adapter_down_factor": adapter_down_factor, "adapter_up_factor": adapter_up_factor, "output_gradient": output_gradient}


@jax.custom_vjp
def low(v):
    return lax.optimization_barrier(v.astype(jnp.bfloat16)).astype(jnp.float32)

@jax.custom_vjp
def low_back(v):
    return v

def low_keep(v):
    return (low(v), None)

def low_pass(kept, grad):
    return (grad,)

def back_keep(v):
    return (v, None)

def back_low(kept, grad):
    return (low(grad),)
low.defvjp(low_keep, low_pass)
low_back.defvjp(back_keep, back_low)
highest = lax.Precision.HIGHEST

def product(left, right):
    return jnp.dot(left, right, precision=highest)

def both_round(values):
    return low(low_back(values))

def norm_rows(values, gain_row, shift_row):
    center = values - lax.optimization_barrier(jnp.mean(values, -1, keepdims=True))
    spread = lax.optimization_barrier(jnp.mean(center * center, -1, keepdims=True))
    return center * lax.rsqrt(spread + 1e-05) * gain_row + shift_row

def attend_pack(inputs):
    queries, key_rows, value_rows, segment = inputs
    seq_rows, model_width = queries.shape
    head_dim = model_width // HEADS
    queries = queries.reshape(seq_rows, HEADS, head_dim)
    key_rows = key_rows.reshape(seq_rows, HEADS, head_dim)
    value_rows = value_rows.reshape(seq_rows, HEADS, head_dim)
    scores = jnp.einsum('qhd,khd->hqk', queries, key_rows, precision=highest) * (1.0 / math.sqrt(head_dim))
    scores = low_back(scores)
    allowed = segment[:, None] == segment[None, :]
    scores = jnp.where(allowed[None], scores, -1000000000.0)
    weight_bundle = low(jax.nn.softmax(scores, axis=-1))
    mixture = jnp.einsum('hqk,khd->qhd', weight_bundle, value_rows, precision=highest)
    return mixture.reshape(seq_rows, model_width)

def layer_forward(residual_hidden, segments, frozen, adapt_down, adapt_up):
    query_key_value_weight, attention_output_weight, feedforward_up_weight, feedforward_down_weight, biases, gains, shifts = frozen
    rows_all, model_width = residual_hidden.shape
    packs_here, seq_rows = segments.shape
    hidden_width = feedforward_up_weight.shape[1]
    rounded = low(residual_hidden)
    joint = product(rounded, query_key_value_weight)
    low_query = both_round(product(rounded, adapt_down[0]))
    low_value = both_round(product(rounded, adapt_down[1]))
    queries = both_round(joint[:, :model_width] + biases[:model_width] + 2.0 * product(low_query, adapt_up[0]))
    key_rows = both_round(joint[:, model_width:2 * model_width])
    value_rows = both_round(joint[:, 2 * model_width:] + biases[model_width:2 * model_width] + 2.0 * product(low_value, adapt_up[1]))

    def by_pack(values):
        return values.reshape(packs_here, seq_rows, model_width)
    attended = lax.map(jax.checkpoint(attend_pack), (by_pack(queries), by_pack(key_rows), by_pack(value_rows), segments))
    context = both_round(attended.reshape(rows_all, model_width))
    branch = low_back(product(context, attention_output_weight) + biases[2 * model_width:3 * model_width])
    normed = norm_rows(residual_hidden + branch, gains[0], shifts[0])
    hidden_pre = low_back(product(low(normed), feedforward_up_weight) + biases[3 * model_width:3 * model_width + hidden_width])
    hidden = low(jax.nn.gelu(hidden_pre, approximate=False))
    ff_out = low_back(product(hidden, feedforward_down_weight) + biases[3 * model_width + hidden_width:])
    return norm_rows(normed + ff_out, gains[1], shifts[1])

def reference(tokens, segment_index_rows, query_key_value_weight, attention_output_weight, feedforward_up_weight, feedforward_down_weight, fixed_bias_stack, layer_norm_gains, layer_norm_shifts, adapter_down_factor, adapter_up_factor, output_gradient):
    frozen = [tuple((array[current_layer_index].astype(jnp.float32) for array in (query_key_value_weight, attention_output_weight, feedforward_up_weight, feedforward_down_weight, fixed_bias_stack, layer_norm_gains, layer_norm_shifts))) for current_layer_index in range(ENCODER_LAYERS)]
    group_size = math.gcd(PACKS, 8)
    group_count = PACKS // group_size
    group_rows = group_size * SEQ
    blocks_all = (tokens.astype(jnp.float32).reshape(group_count, group_rows, MODEL_DIMENSION), segment_index_rows.reshape(group_count, group_size, SEQ), output_gradient.astype(jnp.float32).reshape(group_count, group_rows, MODEL_DIMENSION))
    down_projection_float = adapter_down_factor.astype(jnp.float32)
    up_projection_float = adapter_up_factor.astype(jnp.float32)

    def scan_step(carry, item):
        block_rows, segments, cotangent = item

        def run_layers(residual_hidden, adapt_down, adapt_up):
            for current_layer_index in range(ENCODER_LAYERS):
                residual_hidden = layer_forward(residual_hidden, segments, frozen[current_layer_index], adapt_down[current_layer_index], adapt_up[current_layer_index])
            return residual_hidden
        result, pullback = jax.vjp(run_layers, block_rows, down_projection_float, up_projection_float)
        grad_stream, grad_adapt_down, grad_adapt_up = pullback(cotangent)
        return ((carry[0] + grad_adapt_down, carry[1] + grad_adapt_up), (result, grad_stream))
    zero_sums = (jnp.zeros(down_projection_float.shape, jnp.float32), jnp.zeros(up_projection_float.shape, jnp.float32))
    totals, (outputs, gradients) = lax.scan(scan_step, zero_sums, blocks_all)
    return (outputs.reshape(TOKENS, MODEL_DIMENSION).astype(jnp.bfloat16), gradients.reshape(TOKENS, MODEL_DIMENSION).astype(jnp.bfloat16), totals[0], totals[1])
```

```python
import functools
import types

import jax
import jax.numpy as jnp
from jax import lax
from jax.experimental import pallas as pl
from jax.experimental.pallas import tpu as pltpu
from jax.sharding import PartitionSpec as P

HEADS = 12
BF = jnp.bfloat16
F32 = jnp.float32
MESH = pl.DeviceIdType.MESH
VMEM_BYTES = 63 << 20
SMALL_ROWS = 32
FAR = -(2.0**30)
PIECE_US = 16.5
OWN_AT = -12.0
STAGE_AT = (0.0, 5.0, 10.0, 16.0, 19.0, 23.0)


def dot(left, right, left_dim, right_dim):
    return lax.dot_general(
        left, right, (((left_dim,), (right_dim,)), ((), ())), preferred_element_type=F32
    )


def tile16(value):
    return pl.multiple_of(value, 16)


def picker(rows, columns, start):
    down = lax.broadcasted_iota(jnp.int32, (rows, columns), 0)
    across = lax.broadcasted_iota(jnp.int32, (rows, columns), 1)
    return (down == across + start).astype(F32).astype(BF)


class Gather:
    ZC, X, Y, ZE, ZF, XB, XF, YA, YE = range(9)

    def __init__(self, blocks, arrive_sem, sibling_sem, send_sem):
        self.blocks, self.arrive, self.sibling, self.send = blocks, arrive_sem, sibling_sem, send_sem
        wide = lax.axis_index("wide")
        self.y = lax.axis_index("narrow")
        self.c = lax.rem(wide, 2)
        self.x = lax.rem(wide // 2, 2)
        self.z = wide // 4
        self.rows = blocks.shape[2]

    def device(self, x, y, z, c):
        return (z * 4 + x * 2 + c, y)

    def index(self, x, y, z, c):
        return z * 8 + x * 4 + c * 2 + y

    def barrier(self):
        entry = pltpu.get_barrier_semaphore()
        x, y, z, c = self.x, self.y, self.z, self.c
        for to in (self.to_x(), self.to_y(), (x, y, z, 1 - c)):
            pl.semaphore_signal(entry, inc=1, device_id=self.device(*to), device_id_type=MESH)
        for step in (-1, 1):
            self.onward(
                step,
                lambda: pl.semaphore_signal(
                    entry, inc=1, device_id=self.device(*self.to_z(step)), device_id_type=MESH
                ),
            )
        pl.semaphore_wait(entry, jnp.where(jnp.logical_and(self.z > 0, self.z < 3), 5, 4))

    def to_x(self):
        return (1 - self.x, self.y, self.z, self.c)

    def to_y(self):
        return (self.x, 1 - self.y, self.z, self.c)

    def to_z(self, step):
        return (self.x, self.y, self.z + step, self.c)

    def onward(self, step, act):
        pl.when(jnp.logical_and(self.z + step >= 0, self.z + step <= 3))(act)

    def part(self, k, source, low, high):
        return self.blocks.at[k, self.index(*source), pl.ds(low, high - low)]

    def push(self, k, source, low, high, to, sem):
        ref = self.part(k, source, low, high)
        pltpu.make_async_remote_copy(
            src_ref=ref,
            dst_ref=ref,
            send_sem=self.send,
            recv_sem=sem,
            device_id=self.device(*to),
            device_id_type=MESH,
        ).start()

    def got(self, k, source, low, high, sem):
        ref = self.part(k, source, low, high)
        pltpu.make_async_copy(ref, ref, sem).wait()

    def sem(self, k, kind, source_z):
        return self.arrive.at[k, kind, source_z]

    def to_sibling(self, k, source):
        x, y, z, _ = source
        to = (self.x, self.y, self.z, 1 - self.c)
        self.push(k, source, 0, 96, to, self.sibling.at[k, z * 4 + x * 2 + y])

    def own(self, k):
        me = (self.x, self.y, self.z, self.c)
        self.push(k, me, 0, 96, self.to_x(), self.sem(k, self.X, self.z))
        self.push(k, me, 0, 96, self.to_y(), self.sem(k, self.Y, self.z))
        for step in (-1, 1):
            self.onward(
                step,
                lambda: self.push(
                    k, me, 0, 96, self.to_z(step), self.sem(k, self.ZC, self.z)
                ),
            )
        self.to_sibling(k, me)

    def both(self, distance, act):
        for step in (-1, 1):
            source_z = self.z + step * distance
            there = jnp.logical_and(source_z >= 0, source_z <= 3)
            yield functools.partial(pl.when(there), functools.partial(act, -step, source_z))

    def column(self, k, distance):
        def act(step, zs):
            source = (self.x, self.y, zs, self.c)
            self.got(k, source, 0, 96, self.sem(k, self.ZC, zs))
            self.onward(
                step,
                lambda: self.push(k, source, 0, 96, self.to_z(step), self.sem(k, self.ZC, zs)),
            )
            self.push(k, source, 32, 96, self.to_x(), self.sem(k, self.X, zs))
            self.push(k, source, 0, 64, self.to_y(), self.sem(k, self.Y, zs))
            self.to_sibling(k, source)

        return list(self.both(distance, act))

    def direct(self, k):
        def from_x():
            source = (1 - self.x, self.y, self.z, self.c)
            self.got(k, source, 0, 96, self.sem(k, self.X, self.z))
            for step in (-1, 1):
                self.onward(
                    step,
                    lambda: self.push(
                        k, source, 0, 32, self.to_z(step), self.sem(k, self.ZE, self.z)
                    ),
                )
            self.push(k, source, 0, 48, self.to_y(), self.sem(k, self.YA, self.z))
            self.to_sibling(k, source)

        def from_y():
            source = (self.x, 1 - self.y, self.z, self.c)
            self.got(k, source, 0, 96, self.sem(k, self.Y, self.z))
            for step in (-1, 1):
                self.onward(
                    step,
                    lambda: self.push(
                        k, source, 64, 96, self.to_z(step), self.sem(k, self.ZF, self.z)
                    ),
                )
            self.push(k, source, 48, 96, self.to_x(), self.sem(k, self.XB, self.z))
            self.to_sibling(k, source)

        return [from_x, from_y]

    def across(self, k, distance):
        def act(step, zs):
            source = (1 - self.x, self.y, zs, self.c)
            self.got(k, source, 32, 96, self.sem(k, self.X, zs))
            self.push(k, source, 32, 48, self.to_y(), self.sem(k, self.YA, zs))
            source = (self.x, 1 - self.y, zs, self.c)
            self.got(k, source, 0, 64, self.sem(k, self.Y, zs))
            self.push(k, source, 48, 64, self.to_x(), self.sem(k, self.XB, zs))

        return list(self.both(distance, act))

    def along(self, k, distance):
        def act(step, zs):
            source = (1 - self.x, self.y, zs, self.c)
            self.got(k, source, 0, 32, self.sem(k, self.ZE, zs))
            self.onward(
                step,
                lambda: self.push(k, source, 0, 32, self.to_z(step), self.sem(k, self.ZE, zs)),
            )
            self.push(k, source, 0, 32, self.to_y(), self.sem(k, self.YE, zs))
            self.to_sibling(k, source)
            other = (self.x, 1 - self.y, zs, self.c)
            self.got(k, other, 64, 96, self.sem(k, self.ZF, zs))
            self.onward(
                step,
                lambda: self.push(k, other, 64, 96, self.to_z(step), self.sem(k, self.ZF, zs)),
            )
            self.push(k, other, 64, 96, self.to_x(), self.sem(k, self.XF, zs))
            self.to_sibling(k, other)

        return list(self.both(distance, act))

    def corner(self, k, distance):
        def here():
            source = (1 - self.x, 1 - self.y, self.z, self.c)
            self.got(k, source, 48, 96, self.sem(k, self.XB, self.z))
            self.got(k, source, 0, 48, self.sem(k, self.YA, self.z))
            self.to_sibling(k, source)

        def act(step, zs):
            source = (1 - self.x, 1 - self.y, zs, self.c)
            self.got(k, source, 48, 64, self.sem(k, self.XB, zs))
            self.got(k, source, 32, 48, self.sem(k, self.YA, zs))
            self.got(k, source, 64, 96, self.sem(k, self.XF, zs))
            self.got(k, source, 0, 32, self.sem(k, self.YE, zs))
            self.to_sibling(k, source)

        return list(self.both(distance, act)) if distance else [here]

    def timetable(self, pieces):
        order = []
        ends = []
        for k in range(pieces):
            start = PIECE_US * k
            stages = [(OWN_AT, [functools.partial(self.own, k)] if k else [])]
            stages += [(STAGE_AT[0], self.column(k, 1) + self.direct(k))]
            stages += [(STAGE_AT[1], self.column(k, 2) + self.across(k, 1) + self.along(k, 1))]
            stages += [(STAGE_AT[2], self.column(k, 3) + self.across(k, 2) + self.along(k, 2) + self.across(k, 3))]
            stages += [(STAGE_AT[3], self.along(k, 3) + self.corner(k, 0) + self.corner(k, 1))]
            stages += [(STAGE_AT[4], self.corner(k, 2) + self.corner(k, 3))]
            for (at, steps), (after, _) in zip(stages, stages[1:] + [(STAGE_AT[5], [])], strict=True):
                for number, step in enumerate(steps):
                    order.append((start + at + (after - at) * number / len(steps), len(order), step))
            ends.append(order[-1][:2])
        order.sort(key=lambda entry: entry[:2])
        return [(when, step) for when, _, step in order], [
            next(i + 1 for i, entry in enumerate(order) if entry[:2] == end) for end in ends
        ]

    def from_sibling(self, k):
        @pl.loop(0, 16)
        def _(i):
            source = (lax.rem(i // 2, 2), lax.rem(i, 2), i // 4, 1 - self.c)
            self.got(k, source, 0, 96, self.sibling.at[k, i])

    def drain(self, pieces):
        assert pieces == 6

        def left(blocks):
            ref = self.blocks.at[0, pl.ds(0, blocks)]
            pltpu.make_async_copy(ref, ref, self.send).wait()

        for _ in range(5):
            left(32)
        left(6)

        @pl.when(jnp.logical_and(self.z > 0, self.z < 3))
        def _():
            left(32)
            left(8)


class Weaver:
    def __init__(self, steps, ends):
        self.steps, self.ends = steps, ends
        self.at, self.clock = 0, 0.0

    def due(self):
        start = self.at
        while self.at < len(self.steps) and self.steps[self.at][0] <= self.clock:
            self.at += 1
        return [step for _, step in self.steps[start : self.at]]

    def until(self, piece):
        if not self.steps:
            return
        for _, step in self.steps[self.at : self.ends[piece]]:
            step()
        self.at = max(self.at, self.ends[piece])
        self.clock = max(self.clock, self.steps[self.ends[piece] - 1][0])

    def spend(self, micros):
        for step in self.due():
            step()
        self.clock += micros

    def loop(self, count, body, micros):
        turns = []
        for _ in range(count):
            turns.append(self.due())
            self.clock += micros

        @pl.loop(0, count)
        def _(i):
            for turn, mine in enumerate(turns):
                if mine:

                    @pl.when(i == turn)
                    def _():
                        for step in mine:
                            step()

            body(i)


def sum_small(gather, small, small_sem, send_sem):
    me = (gather.x, gather.y, gather.z, gather.c)
    sibling = (gather.x, gather.y, gather.z, 1 - gather.c)

    def send(slot, to, into):
        pltpu.make_async_remote_copy(
            src_ref=small.at[slot],
            dst_ref=small.at[into],
            send_sem=send_sem.at[into],
            recv_sem=small_sem.at[into],
            device_id=gather.device(*to),
            device_id_type=MESH,
        ).start()

    def sent(slot):
        pltpu.make_async_copy(small.at[slot], small.at[slot], send_sem.at[slot]).wait()

    def got(slot):
        pltpu.make_async_copy(small.at[slot], small.at[slot], small_sem.at[slot]).wait()

    def first():
        send(0, sibling, 1)

    def second():
        got(1)
        small[2] = small[0] + small[1]
        send(2, gather.to_x(), 3)

    def third():
        got(3)
        small[4] = small[2] + small[3]
        send(4, gather.to_y(), 5)

    def fourth():
        got(5)
        small[6 + gather.z] = small[4] + small[5]
        for step in (-1, 1):
            gather.onward(step, lambda: send_column(step, gather.z))

    def send_column(step, zs):
        slot = 6 + zs
        pltpu.make_async_remote_copy(
            src_ref=small.at[slot],
            dst_ref=small.at[slot],
            send_sem=send_sem.at[6 + (step + 1) // 2],
            recv_sem=small_sem.at[slot],
            device_id=gather.device(*gather.to_z(step)),
            device_id_type=MESH,
        ).start()

    def pass_on(step, zs):
        got(6 + zs)
        gather.onward(step, lambda: send_far(step, zs))

    def send_far(step, zs):
        slot = 6 + zs
        pltpu.make_async_remote_copy(
            src_ref=small.at[slot],
            dst_ref=small.at[slot],
            send_sem=send_sem.at[8 + slot],
            recv_sem=small_sem.at[slot],
            device_id=gather.device(*gather.to_z(step)),
            device_id_type=MESH,
        ).start()

    def wait_far(step, zs):
        gather.onward(step, lambda: sent_as(6 + zs, 8 + 6 + zs))

    def sent_as(slot, sem):
        pltpu.make_async_copy(small.at[slot], small.at[slot], send_sem.at[sem]).wait()

    def last():
        sent(1), sent(3), sent(5)
        for step in (-1, 1):
            gather.onward(step, lambda: sent_as(6, 6 + (step + 1) // 2))
        for distance in (1, 2, 3):
            for act in gather.both(distance, wait_far):
                act()

    steps = [first, second, third, fourth]
    for distance in (1, 2, 3):
        steps += list(gather.both(distance, pass_on))
    return steps, last


def norm_rows(values, gain, shift):
    center = values - jnp.mean(values, -1, keepdims=True)
    inverse = lax.rsqrt(jnp.mean(center * center, -1, keepdims=True) + 1e-05)
    hat = center * inverse
    return hat * gain + shift, hat, inverse


def norm_back(grad, hat, inverse, gain):
    grad_hat = grad * gain
    return inverse * (
        grad_hat
        - jnp.mean(grad_hat, -1, keepdims=True)
        - hat * jnp.mean(grad_hat * hat, -1, keepdims=True)
    )


def place_adapters(layer, down_ref, up_ref, a16t, b2):
    rank, width = down_ref.shape[2:]
    a16t[...] = jnp.concatenate([down_ref[layer, 0].astype(F32), down_ref[layer, 1].astype(F32)], 0).astype(BF)
    b2[...] = jnp.zeros_like(b2)
    b2[0:16, 0:width] = (2.0 * dot(picker(16, rank, 0), up_ref[layer, 0], 1, 0)).astype(BF)
    b2[0:16, 2 * width : 3 * width] = (
        2.0 * dot(picker(16, rank, rank), up_ref[layer, 1], 1, 0)
    ).astype(BF)


def forward_kernel(fast, names_in, names_out, names_scratch, *refs):
    names = names_in + names_out + names_scratch
    r = types.SimpleNamespace(**dict(zip(names, refs, strict=True)))
    blocks, joined = r.blocks, r.joined
    layers, packs_rows, width = 2, r.tokens.shape[0], r.tokens.shape[1]
    triple = 3 * width
    hidden = r.g.shape[1]
    head_dim = width // HEADS
    x, n1, acc, xb, n1b = r.x, r.n1, r.acc, r.xb, r.n1b
    qkvt, ot, probs = r.qkvt, r.ot, r.probs
    pieces = 6
    out_sem = r.out_sem
    waits = []

    def keep(source, target, number):
        copy = pltpu.make_async_copy(source, target, out_sem.at[number])
        copy.start()
        return copy

    if fast:
        gather = Gather(blocks, r.arrive_sem, r.sibling_sem, r.send_sem)
        me = gather.index(gather.x, gather.y, gather.z, gather.c)
        for layer in range(layers):
            both = jnp.concatenate([r.qkv_w[layer].astype(F32), r.o_w[layer].astype(F32)], 0)
            blocks[3 * layer, me] = both.astype(BF)
            blocks[3 * layer + 1, me] = r.up_w[layer]
            blocks[3 * layer + 2, me] = r.down_w[layer]
        small = r.small
        own = jnp.zeros((SMALL_ROWS, width), F32)
        few = r.bias.shape[1]
        per_row = width // few
        spot = picker(width, few, lax.rem(me, per_row) * few)
        thin = r.gains.shape[2]
        thin_spot = picker(width, thin, me * thin)
        row = lax.broadcasted_iota(jnp.int32, (SMALL_ROWS, width), 0)
        spread = dot(r.bias[...], spot, 1, 1)
        for layer in range(layers):
            own = jnp.where(row == 8 * layer + me // per_row, spread[layer : layer + 1], own)
            for kind, name in enumerate(("gains", "shifts")):
                thin_rows = dot(getattr(r, name)[layer], thin_spot, 1, 1)
                for which in range(2):
                    at = 16 + 4 * layer + 2 * kind + which
                    own = jnp.where(row == at, thin_rows[which : which + 1], own)
        small[0] = own.astype(BF)
        gather.barrier()
        small_steps, small_end = sum_small(gather, small, r.small_sem, r.small_send)
        gather.own(0)
        steps, ends = gather.timetable(pieces)
        for number, step in enumerate(small_steps):
            steps.append((1.5 * number, step))
        last_of = [steps[end - 1] for end in ends]
        steps.sort(key=lambda entry: entry[0])
        weaver = Weaver(steps, [steps.index(entry) + 1 for entry in last_of])
        weaver.until(0)
        sums = small[6].astype(F32) + small[7].astype(F32) + small[8].astype(F32) + small[9].astype(F32)
        r.rows[...] = sums
    else:
        for number, piece in enumerate((1, 2, 4, 5)):
            pltpu.make_async_copy(r.ud_in.at[number], blocks.at[piece], r.load_sem.at[piece]).start()
        r.rows[...] = r.small_in[...]
        weaver = Weaver([], [])
    waits.append(keep(r.rows, r.rows_out, 0))

    def arrived(k):
        if fast:
            weaver.until(k)
            gather.from_sibling(k)
            if k % 3 == 0:
                joint = r.qkv_w.shape[1]
                lone = 96 - joint

                @pl.loop(0, 16)
                def _(m):
                    first = blocks[k, 2 * m].astype(F32)
                    second = blocks[k, 2 * m + 1].astype(F32)
                    pair = jnp.concatenate([first[:joint], second[:joint]], 0)
                    joined[pl.ds(tile16(m * 2 * joint), 2 * joint)] = pair.astype(BF)
                    pair = jnp.concatenate([first[joint:], second[joint:]], 0)
                    joined[pl.ds(tile16(triple + m * 2 * lone), 2 * lone)] = pair.astype(BF)

                return keep(joined, r.joined_out.at[k // 3], 1 + k // 3)
            number = 2 * (k // 3) + k % 3 - 1
            return keep(blocks.at[k], r.ud_out.at[number], 3 + number)
        if k % 3 == 0:
            copy = pltpu.make_async_copy(r.joined_in.at[k // 3], joined, r.load_sem.at[k])
            copy.start()
            copy.wait()
        else:
            pltpu.make_async_copy(blocks.at[k], blocks.at[k], r.load_sem.at[k]).wait()
        return None

    def big(k, start, count):
        return blocks[k, pl.ds(start, count)].reshape(count * blocks.shape[2], width)

    segment = r.segment[...]
    ids = lax.broadcasted_iota(jnp.int32, (16, packs_rows), 0)
    same = ids == segment
    r.one_hot[...] = same.astype(F32).astype(BF)
    r.ones[...] = jnp.ones_like(r.ones)
    r.apart[...] = jnp.where(jnp.logical_or(same, ids >= 4), 0.0, FAR).astype(BF)

    x[...] = r.tokens[...].astype(F32)
    xb[...] = r.tokens[...]

    saved = []
    rows = r.rows
    blocks_per = width // blocks.shape[2]

    for layer in range(layers):
        bias = 8 * layer
        norm = 16 + 4 * layer
        base = 3 * layer
        copy = arrived(base)
        if copy is not None:
            joined_copy = copy
        place_adapters(layer, r.down, r.up, r.a16t, r.b2)
        first_row = lax.broadcasted_iota(jnp.int32, (16, width), 0) == 0
        r.b2[16:32, 0:width] = jnp.where(first_row, rows[bias : bias + 1], 0.0).astype(BF)
        r.b2[16:32, 2 * width : triple] = jnp.where(first_row, rows[bias + 1 : bias + 2], 0.0).astype(BF)
        for copy in saved:
            copy.wait()
        saved = []
        ut = r.ut
        ut[0:16] = dot(r.a16t[...], xb[...], 1, 1).astype(BF)
        ut[16:32] = (lax.broadcasted_iota(jnp.int32, (16, packs_rows), 0) == 0).astype(F32).astype(BF)
        saved.append(keep(xb, r.xb_out.at[layer], 8))
        saved.append(keep(ut, r.ut_out.at[layer], 9))

        for which in range(3):
            weaver.spend(1.0)
            here = slice(which * width, (which + 1) * width)
            found = dot(joined[here], xb[...], 1, 1)
            if which != 1:
                found = found + dot(r.b2[:, here], ut[...], 0, 0)
            found = found.astype(BF)
            qkvt[here] = (found.astype(F32) * head_dim**-0.5).astype(BF) if which == 0 else found
        saved.append(keep(qkvt, r.qkvt_out.at[layer], 10))

        slots = probs.shape[0]
        group = slots // 2

        def attend(i):
            for member in range(group):
                j = i * group + member
                at = pl.multiple_of(j * head_dim, head_dim)
                slot = lax.rem(i, 2) * group + member
                queries = jnp.concatenate([qkvt[pl.ds(at, head_dim)], r.one_hot[...]], 0)
                keys = jnp.concatenate([qkvt[pl.ds(width + at, head_dim)], r.apart[...]], 0)
                values = jnp.concatenate([qkvt[pl.ds(2 * width + at, head_dim)], r.ones[...]], 0)
                scores = dot(keys, queries, 0, 0)
                weights = jnp.exp(scores - jnp.max(scores, 0, keepdims=True)).astype(BF)
                copy = pltpu.make_async_copy(probs.at[slot], r.probs_out.at[layer, j], r.probs_sem.at[slot])
                pl.when(i >= 2)(copy.wait)
                probs[slot] = weights
                copy.start()
                mixed = dot(values, weights, 1, 0)
                share = 1.0 / mixed[head_dim : head_dim + 1]
                ot[pl.ds(at, head_dim)] = (mixed[:head_dim] * share).astype(BF)
                r.shares[pl.ds(j, 1)] = share

        weaver.loop(HEADS // group, attend, 0.65 * group)
        for slot in range(slots):
            pltpu.make_async_copy(probs.at[slot], probs.at[slot], r.probs_sem.at[slot]).wait()
        saved.append(keep(ot, r.ot_out.at[layer], 11))
        saved.append(keep(r.shares, r.shares_out.at[layer], 17))

        weaver.spend(1.0)
        acc[...] = dot(ot[...].T, joined[triple : triple + width], 1, 1)
        weaver.spend(0.5)
        values = x[...] + (acc[...] + rows[bias + 2 : bias + 3])
        normed, hat, inverse = norm_rows(values, rows[norm : norm + 1], rows[norm + 2 : norm + 3])
        n1[...] = normed
        n1b[...] = normed.astype(BF)
        r.hat1[...] = hat.astype(BF)
        r.inv1[...] = jnp.broadcast_to(inverse, r.inv1.shape)
        saved.append(keep(r.hat1, r.hat_out.at[layer, 0], 12))
        saved.append(keep(r.inv1, r.inv_out.at[layer, 0], 13))

        copy = arrived(base + 1)
        if copy is not None:
            waits.append(copy)
        chunks = hidden // width

        def raise_up(i):
            columns = pl.ds(pl.multiple_of(i * width, width), width)
            pre = dot(n1b[...], big(base + 1, i * blocks_per, blocks_per), 1, 1) + rows[pl.ds(bias + 3 + i, 1)]
            phi = 0.5 * (1.0 + lax.erf(pre * 0.7071067811865476))
            r.g[:, columns] = (pre * phi).astype(BF)
            r.dg[:, columns] = (phi + pre * 0.3989422804014327 * jnp.exp(-0.5 * pre * pre)).astype(BF)

        weaver.loop(chunks, raise_up, 1.1)
        saved.append(keep(r.dg, r.dg_out.at[layer], 14))

        copy = arrived(base + 2)
        if copy is not None:
            waits.append(copy)

        weaver.spend(2.7)
        acc[...] = dot(r.g[...], blocks[base + 2].reshape(hidden, width), 1, 0)
        weaver.spend(0.5)
        if layer == 0 and fast:
            joined_copy.wait()

        saved.pop(0).wait()

        values = n1[...] + (acc[...] + rows[bias + 7 : bias + 8])
        normed, hat, inverse = norm_rows(values, rows[norm + 1 : norm + 2], rows[norm + 3 : norm + 4])
        x[...] = normed
        xb[...] = normed.astype(BF)
        r.hat2[...] = hat.astype(BF)
        r.inv2[...] = jnp.broadcast_to(inverse, r.inv2.shape)
        saved.append(keep(r.hat2, r.hat_out.at[layer, 1], 15))
        saved.append(keep(r.inv2, r.inv_out.at[layer, 1], 16))

    saved.append(keep(xb, r.block_out, 7))
    if fast:
        saved.append(joined_copy)
        small_end()
        gather.drain(pieces)
    for copy in saved + waits:
        copy.wait()


def backward_kernel(names_in, names_out, names_scratch, *refs):
    r = types.SimpleNamespace(**dict(zip(names_in + names_out + names_scratch, refs, strict=True)))
    layers = 2
    packs_rows, width = r.grad_in.shape
    triple = 3 * width
    hidden = r.dg.shape[2]
    head_dim = width // HEADS
    grad, gz = r.grad, r.gz
    gqkvt, got, probs = r.gqkvt, r.got, r.probs
    slots = probs.shape[0]

    numbers = iter(range(r.load_sem.shape[0]))

    def load(source, target):
        copy = pltpu.make_async_copy(source, target, r.load_sem.at[next(numbers)])
        copy.start()
        return copy

    rows_here, grad_here = load(r.rows_in, r.rows), load(r.grad_in, gz)
    loads = {}
    for layer in (1, 0):
        loads[layer] = types.SimpleNamespace(
            hat2=load(r.hat_in.at[layer, 1], r.hat.at[layer, 1]),
            inv2=load(r.inv_in.at[layer, 1], r.inv.at[layer, 1]),
            wd=load(r.ud_in.at[2 * layer + 1], r.wd.at[layer]),
            dg=load(r.dg_in.at[layer], r.dg.at[layer]),
            wu=load(r.ud_in.at[2 * layer], r.wu.at[layer]),
            hat1=load(r.hat_in.at[layer, 0], r.hat.at[layer, 0]),
            inv1=load(r.inv_in.at[layer, 0], r.inv.at[layer, 0]),
            joined=load(r.joined_in.at[layer], r.joined.at[layer]),
            shares=load(r.shares_in.at[layer], r.shares.at[layer]),
            ot=load(r.ot_in.at[layer], r.ot.at[layer]),
            qkvt=load(r.qkvt_in.at[layer], r.qkvt.at[layer]),
            ut=load(r.ut_in.at[layer], r.ut.at[layer]),
            xb=load(r.xb_in.at[layer], r.xb.at[layer]),
        )

    def fetch(layer, j, slot):
        return pltpu.make_async_copy(r.probs_in.at[layer, j], probs.at[slot], r.probs_sem.at[slot])

    rows = r.rows
    rows_here.wait()
    grad_here.wait()

    grad[...] = gz[...].astype(F32)
    for layer in (1, 0):
        norm = 16 + 4 * layer
        for j in range(slots):
            fetch(layer, j, j).start()
        place_adapters(layer, r.down, r.up, r.a16t, r.b2)
        loads[layer].hat2.wait()
        loads[layer].inv2.wait()

        found = norm_back(
            grad[...], r.hat[layer, 1].astype(F32), r.inv[layer, 1][:, 0:1], rows[norm + 1 : norm + 1 + 1]
        )
        grad[...] = found
        gz[...] = found.astype(BF)
        loads[layer].wd.wait()
        loads[layer].dg.wait()
        blocks_per = width // r.wd.shape[2]

        @pl.loop(0, hidden // width)
        def _(i):
            columns = pl.ds(pl.multiple_of(i * width, width), width)
            matrix = r.wd[layer, pl.ds(i * blocks_per, blocks_per)].reshape(width, width)
            r.ga[:, columns] = (
                dot(gz[...], matrix, 1, 1) * r.dg[layer, :, columns].astype(F32)
            ).astype(BF)

        loads[layer].wu.wait()

        grad[...] += dot(r.ga[...], r.wu[layer].reshape(hidden, width), 1, 0)
        loads[layer].hat1.wait()
        loads[layer].inv1.wait()

        found = norm_back(
            grad[...], r.hat[layer, 0].astype(F32), r.inv[layer, 0][:, 0:1], rows[norm : norm + 1]
        )
        grad[...] = found
        gz[...] = found.astype(BF)
        loads[layer].joined.wait()
        loads[layer].ot.wait()
        loads[layer].qkvt.wait()

        loads[layer].shares.wait()
        outward = dot(r.joined[layer, triple : triple + width], gz[...], 0, 1)
        for j in range(HEADS):
            here = slice(j * head_dim, (j + 1) * head_dim)
            got[here] = (outward[here] * r.shares[layer, j : j + 1]).astype(BF)
        qkvt = r.qkvt.at[layer]

        group = slots // 2

        @pl.loop(0, HEADS // group)
        def _(i):
            for member in range(group):
                j = i * group + member
                at = pl.multiple_of(j * head_dim, head_dim)
                slot = lax.rem(i, 2) * group + member
                queries = qkvt[pl.ds(at, head_dim)]
                keys = qkvt[pl.ds(width + at, head_dim)]
                values = qkvt[pl.ds(2 * width + at, head_dim)]
                outward = got[pl.ds(at, head_dim)]
                mixed = r.ot[layer, pl.ds(at, head_dim)].astype(F32)
                total = jnp.sum(outward.astype(F32) * mixed, 0, keepdims=True)
                fetch(layer, j, slot).wait()
                weights = probs[slot]
                gvt = dot(outward, weights, 1, 1)
                grad_weights = dot(values, outward, 0, 0)
                grad_scores = (weights.astype(F32) * (grad_weights - total)).astype(BF)
                gqt = dot(keys, grad_scores, 1, 0) * head_dim**-0.5
                gkt = dot(queries, grad_scores, 1, 1)
                gqkvt[pl.ds(at, head_dim)] = gqt.astype(BF)
                gqkvt[pl.ds(width + at, head_dim)] = gkt.astype(BF)
                gqkvt[pl.ds(2 * width + at, head_dim)] = gvt.astype(BF)

                @pl.when(i + 2 < HEADS // group)
                def _():
                    fetch(layer, j + slots, slot).start()

        loads[layer].ut.wait()
        loads[layer].xb.wait()
        ut = r.ut[layer, 0:16]
        b2 = r.b2
        low = (
            dot(b2[0:16, 0:width], gqkvt[0:width], 1, 0)
            + dot(b2[0:16, 2 * width : triple], gqkvt[2 * width : triple], 1, 0)
        ).astype(BF)
        upper = lax.broadcasted_iota(jnp.int32, (16, width), 0) < 8
        r.part[32 * layer + 16 : 32 * layer + 32] = 2.0 * jnp.where(
            upper, dot(ut, gqkvt[0:width], 1, 1), dot(ut, gqkvt[2 * width : triple], 1, 1)
        )
        r.part[32 * layer : 32 * layer + 16] = dot(low, r.xb[layer], 1, 0)

        grad[...] += dot(gqkvt[...], r.joined[layer, 0:triple], 0, 0) + dot(low, r.a16t[...], 0, 0)

    r.grad_out[...] = grad[...].astype(BF)


def reduce_kernel(part, total, mine, theirs, y_in, x_in, c_in, column, here, send_sem, recv_sem):
    wide = lax.axis_index("wide")
    y = lax.axis_index("narrow")
    c = lax.rem(wide, 2)
    x = lax.rem(wide // 2, 2)
    z = wide // 4
    half = total.shape[1]
    to_y, to_x, to_c = (wide, 1 - y), (wide + 2 - 4 * x, y), (wide + 1 - 2 * c, y)

    entry = pltpu.get_barrier_semaphore()
    for to in (to_y, to_x, to_c):
        pl.semaphore_signal(entry, inc=1, device_id=to, device_id_type=MESH)
    for step in (1, 2, 3):
        other = lax.rem(z + step, 4)
        pl.semaphore_signal(entry, inc=1, device_id=(wide + 4 * (other - z), y), device_id_type=MESH)
    pl.semaphore_wait(entry, 6)

    def send(source, target, number, to):
        copy = pltpu.make_async_remote_copy(
            src_ref=source,
            dst_ref=target,
            send_sem=send_sem.at[number],
            recv_sem=recv_sem.at[number],
            device_id=to,
            device_id_type=MESH,
        )
        copy.start()
        return copy

    left, right = part[:, :half], part[:, half:]
    mine[...] = jnp.where(y == 0, left, right)
    theirs[...] = jnp.where(y == 0, right, left).astype(BF)
    send(theirs, y_in, 0, to_y).wait()
    mine[...] += y_in[...].astype(F32)
    here[0] = mine[...].astype(BF)
    send(here.at[0], x_in, 1, to_x).wait()
    mine[...] += x_in[...].astype(F32)
    here[1] = mine[...].astype(BF)
    send(here.at[1], c_in, 2, to_c).wait()
    mine[...] += c_in[...].astype(F32)
    here[2] = mine[...].astype(BF)
    copies = []
    for step in (1, 2, 3):
        other = lax.rem(z + step, 4)
        copies.append(send(here.at[2], column.at[step - 1], 2 + step, (wide + 4 * (other - z), y)))
    for copy in copies:
        copy.wait()
    found = mine[...]
    for step in range(3):
        found += column[step].astype(F32)
    total[...] = found


def vmem_whole():
    return pl.BlockSpec(memory_space=pltpu.VMEM)


def anywhere():
    return pl.BlockSpec(memory_space=pl.ANY)


def shape(dims, kind):
    return jax.ShapeDtypeStruct(dims, kind)


def run_kernel(body, inputs, in_vmem, outputs, out_vmem, scratch, params, cost):
    names_in, names_out, names_scratch = tuple(inputs), tuple(outputs), tuple(scratch)
    found = pl.pallas_call(
        functools.partial(body, names_in, names_out, names_scratch),
        out_shape=[outputs[name] for name in names_out],
        in_specs=[vmem_whole() if name in in_vmem else anywhere() for name in names_in],
        out_specs=[vmem_whole() if name in out_vmem else anywhere() for name in names_out],
        scratch_shapes=[scratch[name] for name in names_scratch],
        compiler_params=params,
        cost_estimate=cost,
    )(*inputs.values())
    return dict(zip(names_out, found, strict=True))


def per_device(
    mesh_sizes,
    tokens,
    segment_index_rows,
    query_key_value_weight,
    attention_output_weight,
    feedforward_up_weight,
    feedforward_down_weight,
    fixed_bias_stack,
    layer_norm_gains,
    layer_norm_shifts,
    adapter_down_factor,
    adapter_up_factor,
    output_gradient,
):
    wide, narrow = mesh_sizes
    devices = wide * narrow
    rows, width = tokens.shape
    layers = query_key_value_weight.shape[0]
    hidden = feedforward_up_weight.shape[2] * devices
    triple = query_key_value_weight.shape[2] * devices
    fast = (wide, narrow) == (16, 2)
    axes = ("wide", "narrow")
    groups, group = 32, hidden // 32

    inputs = dict(
        tokens=tokens,
        segment=segment_index_rows,
        down=jnp.swapaxes(adapter_down_factor, 2, 3),
        up=adapter_up_factor,
    )
    if fast:
        inputs |= dict(
            qkv_w=jnp.swapaxes(query_key_value_weight, 1, 2),
            o_w=jnp.swapaxes(attention_output_weight, 1, 2),
            up_w=jnp.swapaxes(feedforward_up_weight, 1, 2),
            down_w=feedforward_down_weight,
            bias=fixed_bias_stack,
            gains=layer_norm_gains,
            shifts=layer_norm_shifts,
        )
        in_vmem = set(inputs)
    else:
        qkv = lax.all_gather(query_key_value_weight, axes, axis=2, tiled=True)
        out = lax.all_gather(attention_output_weight, axes, axis=2, tiled=True)
        up = lax.all_gather(feedforward_up_weight, axes, axis=2, tiled=True)
        down = lax.all_gather(feedforward_down_weight, axes, axis=1, tiled=True)
        biases = lax.all_gather(fixed_bias_stack, axes, axis=1, tiled=True)
        gains = lax.all_gather(layer_norm_gains, axes, axis=2, tiled=True)
        shifts = lax.all_gather(layer_norm_shifts, axes, axis=2, tiled=True)
        joined = jnp.concatenate([jnp.swapaxes(qkv, 1, 2), jnp.swapaxes(out, 1, 2)], 1)
        both = jnp.stack([jnp.swapaxes(up, 1, 2), down], 1)
        few = [biases.reshape(layers * 8, width)]
        for layer in range(layers):
            few += [gains[layer], shifts[layer]]
        few += [jnp.zeros((SMALL_ROWS - 8 * layers - 4 * layers, width), BF)]
        inputs |= dict(
            joined_in=joined,
            ud_in=both.reshape(2 * layers, groups, group, width),
            small_in=jnp.concatenate(few, 0).astype(F32),
        )
        in_vmem = {"tokens", "segment", "down", "up", "small_in"}

    kept = dict(
        rows_out=shape((SMALL_ROWS, width), F32),
        xb_out=shape((layers, rows, width), BF),
        ut_out=shape((layers, 32, rows), BF),
        qkvt_out=shape((layers, triple, rows), BF),
        probs_out=shape((layers, HEADS, rows, rows), BF),
        ot_out=shape((layers, width, rows), BF),
        shares_out=shape((layers, 16, rows), F32),
        hat_out=shape((layers, 2, rows, width), BF),
        inv_out=shape((layers, 2, rows, 128), F32),
        dg_out=shape((layers, rows, hidden), BF),
    )
    outputs = dict(block_out=shape((rows, width), BF)) | kept
    if fast:
        outputs |= dict(
            joined_out=shape((layers, triple + width, width), BF),
            ud_out=shape((2 * layers, groups, group, width), BF),
        )
    dma = pltpu.SemaphoreType.DMA
    scratch = dict(
        blocks=pltpu.VMEM((3 * layers, groups, group, width), BF),
        joined=pltpu.VMEM((triple + width, width), BF),
        rows=pltpu.VMEM((SMALL_ROWS, width), F32),
        x=pltpu.VMEM((rows, width), F32),
        n1=pltpu.VMEM((rows, width), F32),
        acc=pltpu.VMEM((rows, width), F32),
        xb=pltpu.VMEM((rows, width), BF),
        n1b=pltpu.VMEM((rows, width), BF),
        qkvt=pltpu.VMEM((triple, rows), BF),
        ot=pltpu.VMEM((width, rows), BF),
        probs=pltpu.VMEM((4, rows, rows), BF),
        hat1=pltpu.VMEM((rows, width), BF),
        hat2=pltpu.VMEM((rows, width), BF),
        inv1=pltpu.VMEM((rows, 128), F32),
        inv2=pltpu.VMEM((rows, 128), F32),
        g=pltpu.VMEM((rows, hidden), BF),
        dg=pltpu.VMEM((rows, hidden), BF),
        ut=pltpu.VMEM((32, rows), BF),
        a16t=pltpu.VMEM((16, width), BF),
        b2=pltpu.VMEM((32, triple), BF),
        one_hot=pltpu.VMEM((16, rows), BF),
        apart=pltpu.VMEM((16, rows), BF),
        ones=pltpu.VMEM((16, rows), BF),
        shares=pltpu.VMEM((16, rows), F32),
        out_sem=dma((20,)),
        probs_sem=dma((4,)),
    )
    if fast:
        scratch |= dict(
            small=pltpu.VMEM((10, SMALL_ROWS, width), BF),
            arrive_sem=dma((3 * layers, 9, 4)),
            sibling_sem=dma((3 * layers, 16)),
            send_sem=dma,
            small_sem=dma((10,)),
            small_send=dma((18,)),
        )
        params = pltpu.CompilerParams(
            collective_id=0, has_side_effects=True, vmem_limit_bytes=VMEM_BYTES
        )
    else:
        scratch |= dict(load_sem=dma((3 * layers,)))
        params = pltpu.CompilerParams(vmem_limit_bytes=VMEM_BYTES)
    products = 2 * layers * rows * (width * (triple + width + 2 * hidden) + 2 * rows * width)
    cost = pl.CostEstimate(flops=products, bytes_accessed=100 << 20, transcendentals=0)
    forward = run_kernel(
        functools.partial(forward_kernel, fast), inputs, in_vmem, outputs, set(), scratch, params, cost
    )

    inputs = dict(grad_in=output_gradient, down=inputs["down"], up=adapter_up_factor)
    inputs |= {name[:-4] + "_in": forward[name] for name in kept}
    inputs["joined_in"] = forward["joined_out"] if fast else joined
    inputs["ud_in"] = forward["ud_out"] if fast else both.reshape(2 * layers, groups, group, width)
    outputs = dict(grad_out=shape((rows, width), BF), part=shape((32 * layers, width), F32))
    scratch = dict(
        rows=pltpu.VMEM((SMALL_ROWS, width), F32),
        grad=pltpu.VMEM((rows, width), F32),
        gz=pltpu.VMEM((rows, width), BF),
        hat=pltpu.VMEM((layers, 2, rows, width), BF),
        inv=pltpu.VMEM((layers, 2, rows, 128), F32),
        wd=pltpu.VMEM((layers, groups, group, width), BF),
        wu=pltpu.VMEM((layers, groups, group, width), BF),
        dg=pltpu.VMEM((layers, rows, hidden), BF),
        joined=pltpu.VMEM((layers, triple + width, width), BF),
        ot=pltpu.VMEM((layers, width, rows), BF),
        qkvt=pltpu.VMEM((layers, triple, rows), BF),
        ut=pltpu.VMEM((layers, 32, rows), BF),
        xb=pltpu.VMEM((layers, rows, width), BF),
        shares=pltpu.VMEM((layers, 16, rows), F32),
        probs=pltpu.VMEM((4, rows, rows), BF),
        ga=pltpu.VMEM((rows, hidden), BF),
        gqkvt=pltpu.VMEM((triple, rows), BF),
        got=pltpu.VMEM((width, rows), BF),
        a16t=pltpu.VMEM((16, width), BF),
        b2=pltpu.VMEM((32, triple), BF),
        load_sem=dma((28,)),
        probs_sem=dma((4,)),
    )
    params = pltpu.CompilerParams(vmem_limit_bytes=VMEM_BYTES)
    cost = pl.CostEstimate(flops=2 * products, bytes_accessed=100 << 20, transcendentals=0)
    back = run_kernel(
        backward_kernel, inputs, {"down", "up"}, outputs, {"grad_out", "part"}, scratch, params, cost
    )

    part = back["part"]
    if fast:
        half = width // narrow
        total = pl.pallas_call(
            reduce_kernel,
            out_shape=shape((32 * layers, half), F32),
            in_specs=[vmem_whole()],
            out_specs=vmem_whole(),
            scratch_shapes=[
                pltpu.VMEM((32 * layers, half), F32),
                pltpu.VMEM((32 * layers, half), BF),
                pltpu.VMEM((32 * layers, half), BF),
                pltpu.VMEM((32 * layers, half), BF),
                pltpu.VMEM((32 * layers, half), BF),
                pltpu.VMEM((3, 32 * layers, half), BF),
                pltpu.VMEM((3, 32 * layers, half), BF),
                dma((6,)),
                dma((6,)),
            ],
            compiler_params=pltpu.CompilerParams(collective_id=1, has_side_effects=True),
        )(part)
    else:
        total = lax.psum_scatter(part.astype(BF), "narrow", scatter_dimension=1, tiled=True)
        total = lax.psum(total, "wide").astype(F32)
    total = total.reshape(layers, 2, 2, 8, total.shape[1])
    grad_down = jnp.swapaxes(total[:, 0], 2, 3)
    grad_up = total[:, 1]
    return (forward["block_out"], back["grad_out"], grad_down, grad_up)


def solution(mesh):
    placed = (
        P(("wide", "narrow"), None),
        P(("wide", "narrow"), None),
        P(None, None, ("wide", "narrow")),
        P(None, None, ("wide", "narrow")),
        P(None, None, ("wide", "narrow")),
        P(None, ("wide", "narrow"), None),
        P(None, ("wide", "narrow")),
        P(None, None, ("wide", "narrow")),
        P(None, None, ("wide", "narrow")),
        P(),
        P(),
        P(("wide", "narrow"), None),
    )
    return jax.shard_map(
        functools.partial(per_device, (mesh.shape["wide"], mesh.shape["narrow"])),
        mesh=mesh,
        in_specs=placed,
        out_specs=(
            P(("wide", "narrow"), None),
            P(("wide", "narrow"), None),
            P(None, None, "narrow", None),
            P(None, None, None, "narrow"),
        ),
        check_vma=False,
    )
```

```python
import functools
import types

import jax
import jax.numpy as jnp
from jax import lax
from jax.experimental import pallas as pl
from jax.experimental.pallas import tpu as pltpu
from jax.sharding import PartitionSpec as P

HEADS = 12
BF = jnp.bfloat16
F32 = jnp.float32
MESH = pl.DeviceIdType.MESH
VMEM_BYTES = 63 << 20
SMALL_ROWS = 32
FAR = -(2.0**30)
PIECE_US = 16.5
STEP_US = 0.5
OWN_AT = -12.0
DIRECT_AT = 2.5
COLUMN_AT = (0.0, 5.0, 10.0)
ACROSS_AT = (6.3, 11.5, 14.5)
ALONG_AT = (7.7, 13.0, 16.0)
CORNER_AT = (17.0, 18.0, 19.5, 21.5)


def dot(left, right, left_dim, right_dim):
    return lax.dot_general(
        left, right, (((left_dim,), (right_dim,)), ((), ())), preferred_element_type=F32
    )


def tile16(value):
    return pl.multiple_of(value, 16)


def picker(rows, columns, start):
    down = lax.broadcasted_iota(jnp.int32, (rows, columns), 0)
    across = lax.broadcasted_iota(jnp.int32, (rows, columns), 1)
    return (down == across + start).astype(F32).astype(BF)


class Gather:
    ZC, X, Y, ZE, ZF, XB, XF, YA, YE = range(9)

    def __init__(self, blocks, arrive_sem, sibling_sem, send_sem):
        self.blocks, self.arrive, self.sibling, self.send = blocks, arrive_sem, sibling_sem, send_sem
        wide = lax.axis_index("wide")
        self.y = lax.axis_index("narrow")
        self.c = lax.rem(wide, 2)
        self.x = lax.rem(wide // 2, 2)
        self.z = wide // 4
        self.rows = blocks.shape[2]

    def device(self, x, y, z, c):
        return (z * 4 + x * 2 + c, y)

    def index(self, x, y, z, c):
        return z * 8 + x * 4 + c * 2 + y

    def barrier(self):
        entry = pltpu.get_barrier_semaphore()
        x, y, z, c = self.x, self.y, self.z, self.c
        others = [self.to_x(), self.to_y(), (x, y, z, 1 - c), (1 - x, y, z, 1 - c)]
        others += [(x, y, lax.rem(z + step, 4), c) for step in (1, 2, 3)]
        for to in others:
            pl.semaphore_signal(entry, inc=1, device_id=self.device(*to), device_id_type=MESH)
        pl.semaphore_wait(entry, len(others))

    def to_x(self):
        return (1 - self.x, self.y, self.z, self.c)

    def to_y(self):
        return (self.x, 1 - self.y, self.z, self.c)

    def to_z(self, step):
        return (self.x, self.y, self.z + step, self.c)

    def onward(self, step, act):
        pl.when(jnp.logical_and(self.z + step >= 0, self.z + step <= 3))(act)

    def part(self, k, source, low, high):
        return self.blocks.at[k, self.index(*source), pl.ds(low, high - low)]

    def push(self, k, source, low, high, to, sem):
        ref = self.part(k, source, low, high)
        pltpu.make_async_remote_copy(
            src_ref=ref,
            dst_ref=ref,
            send_sem=self.send.at[k],
            recv_sem=sem,
            device_id=self.device(*to),
            device_id_type=MESH,
        ).start()

    def got(self, k, source, low, high, sem):
        ref = self.part(k, source, low, high)
        pltpu.make_async_copy(ref, ref, sem).wait()

    def sem(self, k, kind, source_z):
        return self.arrive.at[k, kind, source_z]

    def to_sibling(self, k, source):
        x, y, z, _ = source
        to = (self.x, self.y, self.z, 1 - self.c)
        self.push(k, source, 0, 96, to, self.sibling.at[k, z * 4 + x * 2 + y])

    def own(self, k):
        me = (self.x, self.y, self.z, self.c)
        self.push(k, me, 0, 96, self.to_x(), self.sem(k, self.X, self.z))
        self.push(k, me, 0, 96, self.to_y(), self.sem(k, self.Y, self.z))
        for step in (-1, 1):
            self.onward(
                step,
                lambda: self.push(
                    k, me, 0, 96, self.to_z(step), self.sem(k, self.ZC, self.z)
                ),
            )
        self.to_sibling(k, me)

    def both(self, distance, act):
        for step in (-1, 1):
            source_z = self.z + step * distance
            there = jnp.logical_and(source_z >= 0, source_z <= 3)
            yield functools.partial(pl.when(there), functools.partial(act, -step, source_z))

    def column(self, k, distance):
        def act(step, zs):
            source = (self.x, self.y, zs, self.c)
            self.got(k, source, 0, 96, self.sem(k, self.ZC, zs))
            self.onward(
                step,
                lambda: self.push(k, source, 0, 96, self.to_z(step), self.sem(k, self.ZC, zs)),
            )
            self.push(k, source, 32, 96, self.to_x(), self.sem(k, self.X, zs))
            self.push(k, source, 0, 64, self.to_y(), self.sem(k, self.Y, zs))
            self.to_sibling(k, source)

        return list(self.both(distance, act))

    def direct(self, k):
        def from_x():
            source = (1 - self.x, self.y, self.z, self.c)
            self.got(k, source, 0, 96, self.sem(k, self.X, self.z))
            for step in (-1, 1):
                self.onward(
                    step,
                    lambda: self.push(
                        k, source, 0, 32, self.to_z(step), self.sem(k, self.ZE, self.z)
                    ),
                )
            self.push(k, source, 0, 48, self.to_y(), self.sem(k, self.YA, self.z))
            self.to_sibling(k, source)

        def from_y():
            source = (self.x, 1 - self.y, self.z, self.c)
            self.got(k, source, 0, 96, self.sem(k, self.Y, self.z))
            for step in (-1, 1):
                self.onward(
                    step,
                    lambda: self.push(
                        k, source, 64, 96, self.to_z(step), self.sem(k, self.ZF, self.z)
                    ),
                )
            self.push(k, source, 48, 96, self.to_x(), self.sem(k, self.XB, self.z))
            self.to_sibling(k, source)

        return [from_x, from_y]

    def across(self, k, distance):
        def act(step, zs):
            source = (1 - self.x, self.y, zs, self.c)
            self.got(k, source, 32, 96, self.sem(k, self.X, zs))
            self.push(k, source, 32, 48, self.to_y(), self.sem(k, self.YA, zs))
            source = (self.x, 1 - self.y, zs, self.c)
            self.got(k, source, 0, 64, self.sem(k, self.Y, zs))
            self.push(k, source, 48, 64, self.to_x(), self.sem(k, self.XB, zs))

        return list(self.both(distance, act))

    def along(self, k, distance):
        def act(step, zs):
            source = (1 - self.x, self.y, zs, self.c)
            self.got(k, source, 0, 32, self.sem(k, self.ZE, zs))
            self.onward(
                step,
                lambda: self.push(k, source, 0, 32, self.to_z(step), self.sem(k, self.ZE, zs)),
            )
            self.push(k, source, 0, 32, self.to_y(), self.sem(k, self.YE, zs))
            self.to_sibling(k, source)
            other = (self.x, 1 - self.y, zs, self.c)
            self.got(k, other, 64, 96, self.sem(k, self.ZF, zs))
            self.onward(
                step,
                lambda: self.push(k, other, 64, 96, self.to_z(step), self.sem(k, self.ZF, zs)),
            )
            self.push(k, other, 64, 96, self.to_x(), self.sem(k, self.XF, zs))
            self.to_sibling(k, other)

        return list(self.both(distance, act))

    def corner(self, k, distance):
        def here():
            source = (1 - self.x, 1 - self.y, self.z, self.c)
            self.got(k, source, 48, 96, self.sem(k, self.XB, self.z))
            self.got(k, source, 0, 48, self.sem(k, self.YA, self.z))
            self.to_sibling(k, source)

        def act(step, zs):
            source = (1 - self.x, 1 - self.y, zs, self.c)
            self.got(k, source, 48, 64, self.sem(k, self.XB, zs))
            self.got(k, source, 32, 48, self.sem(k, self.YA, zs))
            self.got(k, source, 64, 96, self.sem(k, self.XF, zs))
            self.got(k, source, 0, 32, self.sem(k, self.YE, zs))
            self.to_sibling(k, source)

        return list(self.both(distance, act)) if distance else [here]

    def timetable(self, pieces):
        order = []
        for k in range(pieces):
            groups = [(OWN_AT, [functools.partial(self.own, k)] if k else []), (DIRECT_AT, self.direct(k))]
            groups += [(COLUMN_AT[far], self.column(k, far + 1)) for far in range(3)]
            groups += [(ACROSS_AT[far], self.across(k, far + 1)) for far in range(3)]
            groups += [(ALONG_AT[far], self.along(k, far + 1)) for far in range(3)]
            groups += [(CORNER_AT[far], self.corner(k, far)) for far in range(4)]
            for at, steps in groups:
                for number, step in enumerate(steps):
                    order.append((PIECE_US * k + at + STEP_US * number, len(order), k, step))
        order.sort(key=lambda entry: entry[:2])
        ends = [max(i for i, entry in enumerate(order) if entry[2] == k) + 1 for k in range(pieces)]
        return [(when, step) for when, _, _, step in order], ends

    def from_sibling(self, k):
        @pl.loop(0, 16)
        def _(i):
            source = (lax.rem(i // 2, 2), lax.rem(i, 2), i // 4, 1 - self.c)
            self.got(k, source, 0, 96, self.sibling.at[k, i])

    def drain(self, k):
        def left(blocks, rows):
            ref = self.blocks.at[k, pl.ds(0, blocks), pl.ds(0, rows)]
            pltpu.make_async_copy(ref, ref, self.send.at[k]).wait()

        left(27, 96)
        left(1, 64)

        @pl.when(jnp.logical_and(self.z > 0, self.z < 3))
        def _():
            left(6, 96)
            left(1, 64)


class Weaver:
    def __init__(self, steps, ends):
        self.steps, self.ends = steps, ends
        self.at, self.clock = 0, 0.0

    def due(self):
        start = self.at
        while self.at < len(self.steps) and self.steps[self.at][0] <= self.clock:
            self.at += 1
        return [step for _, step in self.steps[start : self.at]]

    def until(self, piece):
        if not self.steps:
            return
        for _, step in self.steps[self.at : self.ends[piece]]:
            step()
        self.at = max(self.at, self.ends[piece])
        self.clock = max(self.clock, self.steps[self.ends[piece] - 1][0])

    def spend(self, micros):
        for step in self.due():
            step()
        self.clock += micros

    def loop(self, count, body, micros):
        turns = []
        for _ in range(count):
            turns.append(self.due())
            self.clock += micros

        @pl.loop(0, count)
        def _(i):
            for turn, mine in enumerate(turns):
                if mine:

                    @pl.when(i == turn)
                    def _():
                        for step in mine:
                            step()

            body(i)


def sum_small(gather, small, small_sem, send_sem):
    me = (gather.x, gather.y, gather.z, gather.c)
    sibling = (gather.x, gather.y, gather.z, 1 - gather.c)

    def send(slot, to, into):
        pltpu.make_async_remote_copy(
            src_ref=small.at[slot],
            dst_ref=small.at[into],
            send_sem=send_sem.at[into],
            recv_sem=small_sem.at[into],
            device_id=gather.device(*to),
            device_id_type=MESH,
        ).start()

    def sent(slot):
        pltpu.make_async_copy(small.at[slot], small.at[slot], send_sem.at[slot]).wait()

    def got(slot):
        pltpu.make_async_copy(small.at[slot], small.at[slot], small_sem.at[slot]).wait()

    def first():
        send(0, sibling, 1)

    def second():
        got(1)
        small[2] = small[0] + small[1]
        send(2, gather.to_x(), 3)

    def third():
        got(3)
        small[4] = small[2] + small[3]
        send(4, gather.to_y(), 5)

    def fourth():
        got(5)
        small[6 + gather.z] = small[4] + small[5]
        for step in (-1, 1):
            gather.onward(step, lambda: send_column(step, gather.z))

    def send_column(step, zs):
        slot = 6 + zs
        pltpu.make_async_remote_copy(
            src_ref=small.at[slot],
            dst_ref=small.at[slot],
            send_sem=send_sem.at[6 + (step + 1) // 2],
            recv_sem=small_sem.at[slot],
            device_id=gather.device(*gather.to_z(step)),
            device_id_type=MESH,
        ).start()

    def pass_on(step, zs):
        got(6 + zs)
        gather.onward(step, lambda: send_far(step, zs))

    def send_far(step, zs):
        slot = 6 + zs
        pltpu.make_async_remote_copy(
            src_ref=small.at[slot],
            dst_ref=small.at[slot],
            send_sem=send_sem.at[8 + slot],
            recv_sem=small_sem.at[slot],
            device_id=gather.device(*gather.to_z(step)),
            device_id_type=MESH,
        ).start()

    def wait_far(step, zs):
        gather.onward(step, lambda: sent_as(6 + zs, 8 + 6 + zs))

    def sent_as(slot, sem):
        pltpu.make_async_copy(small.at[slot], small.at[slot], send_sem.at[sem]).wait()

    def last():
        sent(1), sent(3), sent(5)
        for step in (-1, 1):
            gather.onward(step, lambda: sent_as(6, 6 + (step + 1) // 2))
        for distance in (1, 2, 3):
            for act in gather.both(distance, wait_far):
                act()

    steps = [first, second, third, fourth]
    for distance in (1, 2, 3):
        steps += list(gather.both(distance, pass_on))
    return steps, last


def norm_rows(values, gain, shift):
    center = values - jnp.mean(values, -1, keepdims=True)
    inverse = lax.rsqrt(jnp.mean(center * center, -1, keepdims=True) + 1e-05)
    hat = center * inverse
    return hat * gain + shift, hat, inverse


def norm_back(grad, hat, inverse, gain):
    grad_hat = grad * gain
    return inverse * (
        grad_hat
        - jnp.mean(grad_hat, -1, keepdims=True)
        - hat * jnp.mean(grad_hat * hat, -1, keepdims=True)
    )


def place_adapters(layer, down_ref, up_ref, a16t, b2):
    rank, width = down_ref.shape[2:]
    a16t[...] = jnp.concatenate([down_ref[layer, 0].astype(F32), down_ref[layer, 1].astype(F32)], 0).astype(BF)
    b2[...] = jnp.zeros_like(b2)
    b2[0:16, 0:width] = (2.0 * dot(picker(16, rank, 0), up_ref[layer, 0], 1, 0)).astype(BF)
    b2[0:16, 2 * width : 3 * width] = (
        2.0 * dot(picker(16, rank, rank), up_ref[layer, 1], 1, 0)
    ).astype(BF)


class Exchange:
    def __init__(self, layer, gather, part, half, incoming, sums, send_sem, recv_sem):
        self.layer, self.gather, self.part, self.half = layer, gather, part, half
        self.incoming, self.sums = incoming.at[layer], sums.at[layer]
        self.send_sem, self.recv_sem = send_sem.at[layer], recv_sem.at[layer]
        self.rows = pl.ds(32 * layer, 32)

    def copy(self, source, slot, to):
        return pltpu.make_async_remote_copy(
            src_ref=self.sums.at[source],
            dst_ref=self.incoming.at[slot],
            send_sem=self.send_sem.at[slot],
            recv_sem=self.recv_sem.at[slot],
            device_id=self.gather.device(*to),
            device_id_type=MESH,
        )

    def copies(self, stage):
        g = self.gather
        x, y, z, c = g.x, g.y, g.z, g.c
        if stage == 0:
            return [self.copy(0, 0, g.to_y())]
        if stage == 1:
            places = [(x, y, z, 1 - c), (1 - x, y, z, c), (1 - x, y, z, 1 - c)]
        else:
            places = [(x, y, lax.rem(z + step, 4), c) for step in (1, 2, 3)]
        return [self.copy(stage, 3 * stage - 2 + number, to) for number, to in enumerate(places)]

    def start(self):
        width = self.part.shape[1]
        values = self.part[self.rows]
        left, right = values[:, : width // 2], values[:, width // 2 :]
        first = self.gather.y == 0
        self.half[self.rows] = jnp.where(first, left, right)
        self.sums[0] = jnp.where(first, right, left).astype(BF)
        for copy in self.copies(0):
            copy.start()

    def add(self, stage):
        total = self.half[self.rows]
        for number, copy in enumerate(self.copies(stage)):
            copy.wait_recv()
            total = total + self.incoming[3 * stage - 2 + number if stage else 0].astype(F32)
        return total

    def go_on(self, stage):
        total = self.add(stage)
        self.half[self.rows] = total
        self.sums[stage + 1] = total.astype(BF)
        for copy in self.copies(stage + 1):
            copy.start()

    def finish(self, down, up):
        total = self.add(2)
        down[self.layer] = total[:16]
        up[self.layer] = total[16:]
        for stage in range(3):
            for copy in self.copies(stage):
                copy.wait_send()


def layers_kernel(fast, names_in, names_out, names_scratch, *refs):
    r = types.SimpleNamespace(**dict(zip(names_in + names_out + names_scratch, refs, strict=True)))
    layers = 2
    blocks = r.blocks
    pack_rows, width = r.tokens.shape
    triple, hidden = 3 * width, r.g.shape[1]
    head_dim = width // HEADS
    part_rows = blocks.shape[2]
    per_width = width // part_rows
    pieces = 3 * layers
    x, narrow, rows, probs = r.x, r.narrow, r.rows, r.probs
    inputs = (r.tokens, r.xb)
    slots = probs.shape[0]
    group = slots // 2

    if fast:
        gather = Gather(blocks, r.arrive_sem, r.sibling_sem, r.send_sem)
        me = gather.index(gather.x, gather.y, gather.z, gather.c)
        for layer in range(layers):
            both = jnp.concatenate([r.qkv_w[layer].astype(F32), r.o_w[layer].astype(F32)], 0)
            blocks[3 * layer, me] = both.astype(BF)
        loads = []
        for layer in range(layers):
            for number, source in enumerate((r.up_w, r.down_w)):
                target = blocks.at[3 * layer + 1 + number, me]
                loads.append(pltpu.make_async_copy(source.at[layer], target, r.load_sem.at[len(loads)]))
                loads[-1].start()
        gather.barrier()
        for copy in loads:
            copy.wait()
        gather.own(0)
        small = r.small
        own = jnp.zeros((SMALL_ROWS, width), F32)
        few = r.bias.shape[1]
        per_row = width // few
        spot = picker(width, few, lax.rem(me, per_row) * few)
        thin = r.gains.shape[2]
        thin_spot = picker(width, thin, me * thin)
        row = lax.broadcasted_iota(jnp.int32, (SMALL_ROWS, width), 0)
        spread = dot(r.bias[...], spot, 1, 1)
        for layer in range(layers):
            own = jnp.where(row == 8 * layer + me // per_row, spread[layer : layer + 1], own)
            for kind, values in enumerate((r.gains, r.shifts)):
                thin_rows = dot(values[layer], thin_spot, 1, 1)
                for which in range(2):
                    at = 16 + 4 * layer + 2 * kind + which
                    own = jnp.where(row == at, thin_rows[which : which + 1], own)
        small[0] = own.astype(BF)
        small_steps, small_end = sum_small(gather, small, r.small_sem, r.small_send)
        steps, ends = gather.timetable(pieces)
        last_of = [steps[end - 1] for end in ends]
        steps += [(1.5 * number, step) for number, step in enumerate(small_steps)]
        steps.sort(key=lambda entry: entry[0])
        weaver = Weaver(steps, [steps.index(entry) + 1 for entry in last_of])
        exchanges = [
            Exchange(layer, gather, r.part, r.half, r.incoming, r.sums, r.sum_send, r.sum_recv)
            for layer in range(layers)
        ]
    else:
        for number, piece in enumerate((1, 2, 4, 5)):
            pltpu.make_async_copy(r.ud_in.at[number], blocks.at[piece], r.load_sem.at[piece]).start()
        rows[...] = r.small_in[...]
        weaver = Weaver([], [])

    segment = r.segment[...]
    ids = lax.broadcasted_iota(jnp.int32, (16, pack_rows), 0)
    same = ids == segment
    r.one_hot[...] = same.astype(F32).astype(BF)
    r.ones[...] = jnp.ones_like(r.ones)
    r.apart[...] = jnp.where(jnp.logical_or(same, ids >= 4), 0.0, FAR).astype(BF)
    x[...] = r.tokens[...].astype(F32)
    for layer in range(layers):
        place_adapters(layer, r.down, r.up, r.a16t.at[layer], r.b2.at[layer])
        r.ut[layer, 16:32] = (ids == 0).astype(F32).astype(BF)

    def joined(layer, start, count):
        found = blocks[0, pl.ds(start, count)] if fast and layer else r.joined[pl.ds(start, count)]
        return found.reshape(count * part_rows, width)

    def matrix(k, start, count):
        return blocks[k, pl.ds(start, count)].reshape(count * part_rows, width)

    def arrived(k):
        if not fast:
            if k % 3 == 0:
                copy = pltpu.make_async_copy(r.joined_in.at[k // 3], r.joined, r.load_sem.at[k])
                copy.start()
                copy.wait()
            else:
                pltpu.make_async_copy(blocks.at[k], blocks.at[k], r.load_sem.at[k]).wait()
            return
        weaver.until(k)
        gather.from_sibling(k)
        if k % 3:
            return
        target = r.joined if k == 0 else blocks.at[0]
        joint = r.qkv_w.shape[1]
        if k:
            gather.drain(0)

        @pl.loop(0, 8)
        def _(i):
            found = [blocks[k, 4 * i + member].astype(F32) for member in range(4)]
            wide = jnp.concatenate([block[:joint] for block in found], 0).astype(BF)
            target[pl.ds(3 * i, 3)] = wide.reshape(3, part_rows, width)
            target[24 + i] = jnp.concatenate([block[joint:] for block in found], 0).astype(BF)

    def keep_inverse(layer, which, inverse):
        lane = lax.broadcasted_iota(jnp.int32, r.inv.shape, 1)
        r.inv[...] = jnp.where(lane == 2 * layer + which, inverse, r.inv[...])

    def probs_copy(layer, j, slot, out):
        here, there = probs.at[slot], r.probs_out.at[layer, j]
        return pltpu.make_async_copy(here if out else there, there if out else here, r.probs_sem.at[slot])

    def slope_copy(layer, i, slot, out):
        here, there = r.slopes.at[slot], r.slopes_out.at[layer, i]
        return pltpu.make_async_copy(here if out else there, there if out else here, r.slopes_sem.at[slot])

    for layer in range(layers):
        bias, norm, base = 8 * layer, 16 + 4 * layer, 3 * layer
        qkvt, ot, ut, b2 = r.qkvt.at[layer], r.ot.at[layer], r.ut.at[layer], r.b2.at[layer]
        xb = inputs[layer]
        arrived(base)
        if fast and layer == 0:
            rows[...] = (
                small[6].astype(F32) + small[7].astype(F32) + small[8].astype(F32) + small[9].astype(F32)
            )
        first_row = lax.broadcasted_iota(jnp.int32, (16, width), 0) == 0
        b2[16:32, 0:width] = jnp.where(first_row, rows[bias : bias + 1], 0.0).astype(BF)
        b2[16:32, 2 * width : triple] = jnp.where(first_row, rows[bias + 1 : bias + 2], 0.0).astype(BF)
        ut[0:16] = dot(r.a16t[layer], xb[...], 1, 1).astype(BF)

        for which in range(3):
            weaver.spend(1.0)
            here = slice(which * width, (which + 1) * width)
            found = dot(joined(layer, which * per_width, per_width), xb[...], 1, 1)
            if which != 1:
                found = found + dot(b2[:, here], ut[...], 0, 0)
            found = found.astype(BF)
            qkvt[here] = (found.astype(F32) * head_dim**-0.5).astype(BF) if which == 0 else found

        def attend(i):
            for member in range(group):
                j = i * group + member
                at = pl.multiple_of(j * head_dim, head_dim)
                slot = lax.rem(i, 2) * group + member
                queries = jnp.concatenate([qkvt[pl.ds(at, head_dim)], r.one_hot[...]], 0)
                keys = jnp.concatenate([qkvt[pl.ds(width + at, head_dim)], r.apart[...]], 0)
                values = jnp.concatenate([qkvt[pl.ds(2 * width + at, head_dim)], r.ones[...]], 0)
                scores = dot(keys, queries, 0, 0)
                weights = jnp.exp(scores - jnp.max(scores, 0, keepdims=True)).astype(BF)
                copy = probs_copy(layer, j, slot, True)
                pl.when(i >= 2)(copy.wait)
                probs[slot] = weights
                copy.start()
                mixed = dot(values, weights, 1, 0)
                share = 1.0 / mixed[head_dim : head_dim + 1]
                ot[pl.ds(at, head_dim)] = (mixed[:head_dim] * share).astype(BF)
                r.shares[layer, pl.ds(j, 1)] = share

        weaver.loop(HEADS // group, attend, 0.65 * group)
        for slot in range(slots):
            probs_copy(layer, 0, slot, True).wait()

        weaver.spend(1.0)
        values = dot(ot[...].T, joined(layer, 3 * per_width, per_width), 1, 1)
        values = x[...] + (values + rows[bias + 2 : bias + 3])
        normed, hat, inverse = norm_rows(values, rows[norm : norm + 1], rows[norm + 2 : norm + 3])
        x[...] = normed
        narrow[...] = normed.astype(BF)
        r.hat[layer, 0] = hat.astype(BF)
        keep_inverse(layer, 0, inverse)
        weaver.spend(0.5)
        arrived(base + 1)
        def raise_up(i):
            columns = pl.ds(pl.multiple_of(i * width, width), width)
            pre = dot(narrow[...], matrix(base + 1, i * per_width, per_width), 1, 1) + rows[pl.ds(bias + 3 + i, 1)]
            phi = 0.5 * (1.0 + lax.erf(pre * 0.7071067811865476))
            r.g[:, columns] = (pre * phi).astype(BF)
            slope = (phi + pre * 0.3989422804014327 * jnp.exp(-0.5 * pre * pre)).astype(BF)
            slot = lax.rem(i, 2)
            copy = slope_copy(layer, i, slot, True)
            pl.when(i >= 2)(copy.wait)
            r.slopes[slot] = slope
            copy.start()

        weaver.loop(hidden // width, raise_up, 1.1)
        for slot in range(2):
            slope_copy(layer, 0, slot, True).wait()
        if layer:
            grad_copy = pltpu.make_async_copy(r.grad_in, narrow, r.load_grad)
            grad_copy.start()
        arrived(base + 2)
        weaver.spend(2.7)
        values = dot(r.g[...], matrix(base + 2, 0, 4 * per_width), 1, 0)
        weaver.spend(0.5)
        values = x[...] + (values + rows[bias + 7 : bias + 8])
        normed, hat, inverse = norm_rows(values, rows[norm + 1 : norm + 2], rows[norm + 3 : norm + 4])
        r.hat[layer, 1] = hat.astype(BF)
        keep_inverse(layer, 1, inverse)
        if layer == 0:
            x[...] = normed
            r.xb[...] = normed.astype(BF)
        else:
            r.g[:, 0:width] = normed.astype(BF)

    out_copy = pltpu.make_async_copy(r.g.at[:, pl.ds(0, width)], r.block_out, r.out_sem)
    out_copy.start()
    grad_copy.wait()
    x[...] = narrow[...].astype(F32)

    def fetch_first(layer):
        for j in range(slots):
            probs_copy(layer, j, j, False).start()

    def back_norm(layer, which):
        gain = 16 + 4 * layer + which
        inverse = r.inv[:, 2 * layer + which : 2 * layer + which + 1]
        found = norm_back(x[...], r.hat[layer, which].astype(F32), inverse, rows[gain : gain + 1])
        x[...] = found
        narrow[...] = found.astype(BF)

    for layer in reversed(range(layers)):
        base = 3 * layer
        qkvt, ot, b2 = r.qkvt.at[layer], r.ot.at[layer], r.b2.at[layer]
        fetch_first(layer)
        for slot in range(2):
            slope_copy(layer, slot, slot, False).start()
        back_norm(layer, 1)
        if layer:
            out_copy.wait()

        @pl.loop(0, hidden // width)
        def _(i):
            columns = pl.ds(pl.multiple_of(i * width, width), width)
            found = dot(narrow[...], matrix(base + 2, i * per_width, per_width), 1, 1)
            slot = lax.rem(i, 2)
            slope_copy(layer, i, slot, False).wait()
            r.g[:, columns] = (found * r.slopes[slot].astype(F32)).astype(BF)

            @pl.when(i + 2 < hidden // width)
            def _():
                slope_copy(layer, i + 2, slot, False).start()

        if fast and layer == 0:
            exchanges[1].go_on(0)
        x[...] += dot(r.g[...], matrix(base + 1, 0, 4 * per_width), 1, 0)
        back_norm(layer, 0)
        if fast and layer == 0:
            exchanges[1].go_on(1)
        outward = dot(joined(layer, 3 * per_width, per_width), narrow[...], 0, 1)
        for j in range(HEADS):
            here = slice(j * head_dim, (j + 1) * head_dim)
            piece = outward[here] * r.shares[layer, j : j + 1]
            r.totals[j : j + 1] = jnp.sum(piece * ot[here].astype(F32), 0, keepdims=True)
            ot[here] = piece.astype(BF)

        @pl.loop(0, HEADS // group)
        def _(i):
            for member in range(group):
                j = i * group + member
                at = pl.multiple_of(j * head_dim, head_dim)
                slot = lax.rem(i, 2) * group + member
                queries = qkvt[pl.ds(at, head_dim)]
                keys = qkvt[pl.ds(width + at, head_dim)]
                values = qkvt[pl.ds(2 * width + at, head_dim)]
                outward = ot[pl.ds(at, head_dim)]
                probs_copy(layer, j, slot, False).wait()
                weights = probs[slot]
                gvt = dot(outward, weights, 1, 1)
                grad_weights = dot(values, outward, 0, 0)
                grad_scores = (weights.astype(F32) * (grad_weights - r.totals[pl.ds(j, 1)])).astype(BF)
                gqt = dot(keys, grad_scores, 1, 0) * head_dim**-0.5
                gkt = dot(queries, grad_scores, 1, 1)
                qkvt[pl.ds(at, head_dim)] = gqt.astype(BF)
                qkvt[pl.ds(width + at, head_dim)] = gkt.astype(BF)
                qkvt[pl.ds(2 * width + at, head_dim)] = gvt.astype(BF)

                @pl.when(i + 2 < HEADS // group)
                def _():
                    probs_copy(layer, j + slots, slot, False).start()

        ut = r.ut[layer, 0:16]
        low = (
            dot(b2[0:16, 0:width], qkvt[0:width], 1, 0)
            + dot(b2[0:16, 2 * width : triple], qkvt[2 * width : triple], 1, 0)
        ).astype(BF)
        upper = lax.broadcasted_iota(jnp.int32, (16, width), 0) < 8
        r.part[32 * layer + 16 : 32 * layer + 32] = 2.0 * jnp.where(
            upper, dot(ut, qkvt[0:width], 1, 1), dot(ut, qkvt[2 * width : triple], 1, 1)
        )
        r.part[32 * layer : 32 * layer + 16] = dot(low, inputs[layer][...], 1, 0)
        if fast:
            exchanges[layer].start()
            if layer == 0:
                exchanges[1].finish(r.down_out, r.up_out)
        found = dot(qkvt[0:width], joined(layer, 0, per_width), 0, 0)
        if fast and layer == 0:
            exchanges[0].go_on(0)
        found = found + dot(qkvt[width : triple], joined(layer, per_width, 2 * per_width), 0, 0)
        if fast and layer == 0:
            exchanges[0].go_on(1)
        x[...] += found + dot(low, r.a16t[layer], 0, 0)

    r.g[:, 0:width] = x[...].astype(BF)
    grad_out_copy = pltpu.make_async_copy(r.g.at[:, pl.ds(0, width)], r.grad_out, r.out_sem)
    grad_out_copy.start()
    if fast:
        exchanges[0].finish(r.down_out, r.up_out)
        small_end()
        for k in range(1, pieces):
            gather.drain(k)
    grad_out_copy.wait()


def hand_over(count, *refs):
    for source, target in zip(refs[:count], refs[count:], strict=True):
        target[...] = source[...]


def vmem_whole():
    return pl.BlockSpec(memory_space=pltpu.VMEM)


def anywhere():
    return pl.BlockSpec(memory_space=pl.ANY)


def shape(dims, kind):
    return jax.ShapeDtypeStruct(dims, kind)


def run_kernel(body, inputs, in_vmem, outputs, out_vmem, scratch, params, cost):
    names_in, names_out, names_scratch = tuple(inputs), tuple(outputs), tuple(scratch)
    found = pl.pallas_call(
        functools.partial(body, names_in, names_out, names_scratch),
        out_shape=[outputs[name] for name in names_out],
        in_specs=[vmem_whole() if name in in_vmem else anywhere() for name in names_in],
        out_specs=[vmem_whole() if name in out_vmem else anywhere() for name in names_out],
        scratch_shapes=[scratch[name] for name in names_scratch],
        compiler_params=params,
        cost_estimate=cost,
    )(*inputs.values())
    return dict(zip(names_out, found, strict=True))


def per_device(
    mesh_sizes,
    tokens,
    segment_index_rows,
    query_key_value_weight,
    attention_output_weight,
    feedforward_up_weight,
    feedforward_down_weight,
    fixed_bias_stack,
    layer_norm_gains,
    layer_norm_shifts,
    adapter_down_factor,
    adapter_up_factor,
    output_gradient,
):
    wide, narrow = mesh_sizes
    devices = wide * narrow
    rows, width = tokens.shape
    layers = query_key_value_weight.shape[0]
    hidden = feedforward_up_weight.shape[2] * devices
    triple = query_key_value_weight.shape[2] * devices
    fast = (wide, narrow) == (16, 2)
    axes = ("wide", "narrow")
    groups, group = 32, hidden // 32

    inputs = dict(
        tokens=tokens,
        segment=segment_index_rows,
        down=jnp.swapaxes(adapter_down_factor, 2, 3),
        up=adapter_up_factor,
    )
    if fast:
        inputs |= dict(
            qkv_w=jnp.swapaxes(query_key_value_weight, 1, 2),
            o_w=jnp.swapaxes(attention_output_weight, 1, 2),
            up_w=jnp.swapaxes(feedforward_up_weight, 1, 2),
            down_w=feedforward_down_weight,
            bias=fixed_bias_stack,
            gains=layer_norm_gains,
            shifts=layer_norm_shifts,
        )
        in_vmem = set(inputs) - {"up_w", "down_w"}
    else:
        qkv = lax.all_gather(query_key_value_weight, axes, axis=2, tiled=True)
        out = lax.all_gather(attention_output_weight, axes, axis=2, tiled=True)
        up = lax.all_gather(feedforward_up_weight, axes, axis=2, tiled=True)
        down = lax.all_gather(feedforward_down_weight, axes, axis=1, tiled=True)
        biases = lax.all_gather(fixed_bias_stack, axes, axis=1, tiled=True)
        gains = lax.all_gather(layer_norm_gains, axes, axis=2, tiled=True)
        shifts = lax.all_gather(layer_norm_shifts, axes, axis=2, tiled=True)
        joined = jnp.concatenate([jnp.swapaxes(qkv, 1, 2), jnp.swapaxes(out, 1, 2)], 1)
        both = jnp.stack([jnp.swapaxes(up, 1, 2), down], 1)
        few = [biases.reshape(layers * 8, width)]
        for layer in range(layers):
            few += [gains[layer], shifts[layer]]
        few += [jnp.zeros((SMALL_ROWS - 12 * layers, width), BF)]
        in_vmem = set(inputs) | {"small_in"}
        inputs |= dict(
            joined_in=joined.reshape(layers, 4 * width // group, group, width),
            ud_in=both.reshape(2 * layers, groups, group, width),
            small_in=jnp.concatenate(few, 0).astype(F32),
        )
    inputs |= dict(grad_in=output_gradient)

    half = width // narrow
    outputs = dict(
        block_out=shape((rows, width), BF),
        grad_out=shape((rows, width), BF),
        probs_out=shape((layers, HEADS, rows, rows), BF),
        slopes_out=shape((layers, hidden // width, rows, width), BF),
    )
    dma = pltpu.SemaphoreType.DMA
    scratch = dict(
        blocks=pltpu.VMEM((3 * layers, groups, group, width), BF),
        joined=pltpu.VMEM((groups, group, width), BF),
        rows=pltpu.VMEM((SMALL_ROWS, width), F32),
        x=pltpu.VMEM((rows, width), F32),
        xb=pltpu.VMEM((rows, width), BF),
        narrow=pltpu.VMEM((rows, width), BF),
        qkvt=pltpu.VMEM((layers, triple, rows), BF),
        ot=pltpu.VMEM((layers, width, rows), BF),
        shares=pltpu.VMEM((layers, 16, rows), F32),
        totals=pltpu.VMEM((16, rows), F32),
        probs=pltpu.VMEM((4, rows, rows), BF),
        hat=pltpu.VMEM((layers, 2, rows, width), BF),
        inv=pltpu.VMEM((rows, 128), F32),
        g=pltpu.VMEM((rows, hidden), BF),
        slopes=pltpu.VMEM((2, rows, width), BF),
        ut=pltpu.VMEM((layers, 32, rows), BF),
        a16t=pltpu.VMEM((layers, 16, width), BF),
        b2=pltpu.VMEM((layers, 32, triple), BF),
        one_hot=pltpu.VMEM((16, rows), BF),
        apart=pltpu.VMEM((16, rows), BF),
        ones=pltpu.VMEM((16, rows), BF),
        probs_sem=dma((4,)),
        slopes_sem=dma((2,)),
        load_grad=dma,
        out_sem=dma,
    )
    if fast:
        outputs |= dict(
            down_out=shape((layers, 16, half), F32),
            up_out=shape((layers, 16, half), F32),
        )
        out_vmem = {"down_out", "up_out"}
        scratch |= dict(
            part=pltpu.VMEM((32 * layers, width), F32),
            half=pltpu.VMEM((32 * layers, half), F32),
            incoming=pltpu.VMEM((layers, 7, 32, half), BF),
            sums=pltpu.VMEM((layers, 3, 32, half), BF),
            sum_send=dma((layers, 7)),
            sum_recv=dma((layers, 7)),
            small=pltpu.VMEM((10, SMALL_ROWS, width), BF),
            arrive_sem=dma((3 * layers, 9, 4)),
            sibling_sem=dma((3 * layers, 16)),
            send_sem=dma((3 * layers,)),
            small_sem=dma((10,)),
            small_send=dma((18,)),
            load_sem=dma((4,)),
        )
        params = pltpu.CompilerParams(
            collective_id=0, has_side_effects=True, vmem_limit_bytes=VMEM_BYTES
        )
    else:
        outputs |= dict(part=shape((32 * layers, width), F32))
        out_vmem = {"part"}
        scratch |= dict(load_sem=dma((3 * layers,)))
        params = pltpu.CompilerParams(vmem_limit_bytes=VMEM_BYTES)
    products = layers * rows * (width * (triple + width + 2 * hidden) * 2 + 7 * rows * width)
    cost = pl.CostEstimate(flops=2 * products, bytes_accessed=100 << 20, transcendentals=0)
    found = run_kernel(
        functools.partial(layers_kernel, fast), inputs, in_vmem, outputs, out_vmem, scratch, params, cost
    )
    if fast:
        results = [found["block_out"], found["grad_out"], found["down_out"], found["up_out"]]
        results = pl.pallas_call(
            functools.partial(hand_over, 4),
            out_shape=[shape(value.shape, value.dtype) for value in results],
            in_specs=[vmem_whole()] * 4,
            out_specs=[vmem_whole()] * 4,
        )(*results)
    else:
        total = lax.psum_scatter(found["part"].astype(BF), "narrow", scatter_dimension=1, tiled=True)
        total = lax.psum(total, "wide").astype(F32).reshape(layers, 2, 16, half)
        results = [found["block_out"], found["grad_out"], total[:, 0], total[:, 1]]
    block_out, grad_out, down_sum, up_sum = results
    grad_down = jnp.swapaxes(down_sum.reshape(layers, 2, 8, half), 2, 3)
    grad_up = up_sum.reshape(layers, 2, 8, half)
    return (block_out, grad_out, grad_down, grad_up)


def solution(mesh):
    placed = (
        P(("wide", "narrow"), None),
        P(("wide", "narrow"), None),
        P(None, None, ("wide", "narrow")),
        P(None, None, ("wide", "narrow")),
        P(None, None, ("wide", "narrow")),
        P(None, ("wide", "narrow"), None),
        P(None, ("wide", "narrow")),
        P(None, None, ("wide", "narrow")),
        P(None, None, ("wide", "narrow")),
        P(),
        P(),
        P(("wide", "narrow"), None),
    )
    return jax.shard_map(
        functools.partial(per_device, (mesh.shape["wide"], mesh.shape["narrow"])),
        mesh=mesh,
        in_specs=placed,
        out_specs=(
            P(("wide", "narrow"), None),
            P(("wide", "narrow"), None),
            P(None, None, "narrow", None),
            P(None, None, None, "narrow"),
        ),
        check_vma=False,
    )
```

```python
import functools
import types

import jax
import jax.numpy as jnp
from jax import lax
from jax.experimental import pallas as pl
from jax.experimental.pallas import tpu as pltpu
from jax.sharding import PartitionSpec as P

HEADS = 12
BF = jnp.bfloat16
F32 = jnp.float32
MESH = pl.DeviceIdType.MESH
VMEM_BYTES = 63 << 20
SMALL_ROWS = 32
FAR = -(2.0**30)
GROUP = 4
LEAD_US = 2.0
WHEN = tuple(
    tuple(
        16.5 * k + at
        for at in (-12.0, 2.5, 3.0, 0.0, 0.5, 5.0, 5.5, 10.0, 10.5, 6.3, 6.8, 11.5, 12.0, 14.5, 15.0, 7.7, 8.2, 13.0, 13.5, 16.0, 16.5)
        + (18.0, 18.5, 19.5, 20.0, 21.5, 22.0, 17.0)
    )
    for k in range(6)
)


def dot(left, right, left_dim, right_dim):
    return lax.dot_general(
        left, right, (((left_dim,), (right_dim,)), ((), ())), preferred_element_type=F32
    )


def tile16(value):
    return pl.multiple_of(value, 16)


def picker(rows, columns, start):
    down = lax.broadcasted_iota(jnp.int32, (rows, columns), 0)
    across = lax.broadcasted_iota(jnp.int32, (rows, columns), 1)
    return (down == across + start).astype(F32).astype(BF)


class Gather:
    ZC, X, Y, ZE, ZF, XB, XF, YA, YE = range(9)

    def __init__(self, blocks, arrive_sem, sibling_sem, send_sem):
        self.blocks, self.arrive, self.sibling, self.send = blocks, arrive_sem, sibling_sem, send_sem
        wide = lax.axis_index("wide")
        self.y = lax.axis_index("narrow")
        self.c = lax.rem(wide, 2)
        self.x = lax.rem(wide // 2, 2)
        self.z = wide // 4
        self.rows = blocks.shape[2]

    def device(self, x, y, z, c):
        return (z * 4 + x * 2 + c, y)

    def index(self, x, y, z, c):
        return z * 8 + x * 4 + c * 2 + y

    def greet(self):
        entry = pltpu.get_barrier_semaphore()
        x, y, z, c = self.x, self.y, self.z, self.c
        others = [self.to_x(), self.to_y(), (x, y, z, 1 - c), (1 - x, y, z, 1 - c)]
        others += [(x, y, lax.rem(z + step, 4), c) for step in (1, 2, 3)]
        for to in others:
            pl.semaphore_signal(entry, inc=1, device_id=self.device(*to), device_id_type=MESH)
        return len(others)

    def to_x(self):
        return (1 - self.x, self.y, self.z, self.c)

    def to_y(self):
        return (self.x, 1 - self.y, self.z, self.c)

    def to_z(self, step):
        return (self.x, self.y, self.z + step, self.c)

    def onward(self, step, act):
        pl.when(jnp.logical_and(self.z + step >= 0, self.z + step <= 3))(act)

    def part(self, k, source, low, high):
        return self.blocks.at[k, self.index(*source), pl.ds(low, high - low)]

    def push(self, k, source, low, high, to, sem):
        ref = self.part(k, source, low, high)
        pltpu.make_async_remote_copy(
            src_ref=ref,
            dst_ref=ref,
            send_sem=self.send.at[k],
            recv_sem=sem,
            device_id=self.device(*to),
            device_id_type=MESH,
        ).start()

    def got(self, k, source, low, high, sem):
        ref = self.part(k, source, low, high)
        pltpu.make_async_copy(ref, ref, sem).wait()

    def sem(self, k, kind, source_z):
        return self.arrive.at[k, kind, source_z]

    def to_sibling(self, k, source):
        x, y, z, _ = source
        to = (self.x, self.y, self.z, 1 - self.c)
        self.push(k, source, 0, 96, to, self.sibling.at[k, z * 4 + x * 2 + y])

    def own(self, k):
        me = (self.x, self.y, self.z, self.c)
        self.push(k, me, 0, 96, self.to_x(), self.sem(k, self.X, self.z))
        self.push(k, me, 0, 96, self.to_y(), self.sem(k, self.Y, self.z))
        for step in (-1, 1):
            self.onward(
                step,
                lambda: self.push(
                    k, me, 0, 96, self.to_z(step), self.sem(k, self.ZC, self.z)
                ),
            )
        self.to_sibling(k, me)

    def both(self, distance, act):
        for step in (-1, 1):
            source_z = self.z + step * distance
            there = jnp.logical_and(source_z >= 0, source_z <= 3)
            yield functools.partial(pl.when(there), functools.partial(act, -step, source_z))

    def column(self, k, distance):
        def act(step, zs):
            source = (self.x, self.y, zs, self.c)
            self.got(k, source, 0, 96, self.sem(k, self.ZC, zs))
            self.onward(
                step,
                lambda: self.push(k, source, 0, 96, self.to_z(step), self.sem(k, self.ZC, zs)),
            )
            self.push(k, source, 32, 96, self.to_x(), self.sem(k, self.X, zs))
            self.push(k, source, 0, 64, self.to_y(), self.sem(k, self.Y, zs))
            self.to_sibling(k, source)

        return list(self.both(distance, act))

    def direct(self, k):
        def from_x():
            source = (1 - self.x, self.y, self.z, self.c)
            self.got(k, source, 0, 96, self.sem(k, self.X, self.z))
            for step in (-1, 1):
                self.onward(
                    step,
                    lambda: self.push(
                        k, source, 0, 32, self.to_z(step), self.sem(k, self.ZE, self.z)
                    ),
                )
            self.push(k, source, 0, 48, self.to_y(), self.sem(k, self.YA, self.z))
            self.to_sibling(k, source)

        def from_y():
            source = (self.x, 1 - self.y, self.z, self.c)
            self.got(k, source, 0, 96, self.sem(k, self.Y, self.z))
            for step in (-1, 1):
                self.onward(
                    step,
                    lambda: self.push(
                        k, source, 64, 96, self.to_z(step), self.sem(k, self.ZF, self.z)
                    ),
                )
            self.push(k, source, 48, 96, self.to_x(), self.sem(k, self.XB, self.z))
            self.to_sibling(k, source)

        return [from_x, from_y]

    def across(self, k, distance):
        def act(step, zs):
            source = (1 - self.x, self.y, zs, self.c)
            self.got(k, source, 32, 96, self.sem(k, self.X, zs))
            self.push(k, source, 32, 48, self.to_y(), self.sem(k, self.YA, zs))
            source = (self.x, 1 - self.y, zs, self.c)
            self.got(k, source, 0, 64, self.sem(k, self.Y, zs))
            self.push(k, source, 48, 64, self.to_x(), self.sem(k, self.XB, zs))

        return list(self.both(distance, act))

    def along(self, k, distance):
        def act(step, zs):
            source = (1 - self.x, self.y, zs, self.c)
            self.got(k, source, 0, 32, self.sem(k, self.ZE, zs))
            self.onward(
                step,
                lambda: self.push(k, source, 0, 32, self.to_z(step), self.sem(k, self.ZE, zs)),
            )
            self.push(k, source, 0, 32, self.to_y(), self.sem(k, self.YE, zs))
            self.to_sibling(k, source)
            other = (self.x, 1 - self.y, zs, self.c)
            self.got(k, other, 64, 96, self.sem(k, self.ZF, zs))
            self.onward(
                step,
                lambda: self.push(k, other, 64, 96, self.to_z(step), self.sem(k, self.ZF, zs)),
            )
            self.push(k, other, 64, 96, self.to_x(), self.sem(k, self.XF, zs))
            self.to_sibling(k, other)

        return list(self.both(distance, act))

    def corner(self, k, distance):
        def here():
            source = (1 - self.x, 1 - self.y, self.z, self.c)
            self.got(k, source, 48, 96, self.sem(k, self.XB, self.z))
            self.got(k, source, 0, 48, self.sem(k, self.YA, self.z))
            self.to_sibling(k, source)

        def act(step, zs):
            source = (1 - self.x, 1 - self.y, zs, self.c)
            self.got(k, source, 48, 64, self.sem(k, self.XB, zs))
            self.got(k, source, 32, 48, self.sem(k, self.YA, zs))
            self.got(k, source, 64, 96, self.sem(k, self.XF, zs))
            self.got(k, source, 0, 32, self.sem(k, self.YE, zs))
            self.to_sibling(k, source)

        return list(self.both(distance, act)) if distance else [here]

    def timetable(self, pieces):
        order = []
        for k in range(pieces):
            steps = [functools.partial(self.own, k)] + self.direct(k)
            for group in (self.column, self.across, self.along, self.corner):
                for far in (1, 2, 3):
                    steps += group(k, far)
            steps += self.corner(k, 0)
            for at, step in zip(WHEN[k], steps, strict=True):
                if k or step is not steps[0]:
                    order.append((at, len(order), k, step))
        order.sort(key=lambda entry: entry[:2])
        ends = [max(i for i, entry in enumerate(order) if entry[2] == k) + 1 for k in range(pieces)]
        return [(when, step) for when, _, _, step in order], ends

    def from_sibling(self, k):
        @pl.loop(0, 16)
        def _(i):
            source = (lax.rem(i // 2, 2), lax.rem(i, 2), i // 4, 1 - self.c)
            self.got(k, source, 0, 96, self.sibling.at[k, i])

    def drain(self, k):
        def left(blocks, rows):
            ref = self.blocks.at[k, pl.ds(0, blocks), pl.ds(0, rows)]
            pltpu.make_async_copy(ref, ref, self.send.at[k]).wait()

        left(27, 96)
        left(1, 64)

        @pl.when(jnp.logical_and(self.z > 0, self.z < 3))
        def _():
            left(6, 96)
            left(1, 64)


class Weaver:
    def __init__(self, steps, ends):
        self.steps, self.ends = steps, ends
        self.at, self.clock = 0, 0.0

    def due(self):
        start = self.at
        while self.at < len(self.steps) and self.steps[self.at][0] <= self.clock + LEAD_US:
            self.at += 1
        return [step for _, step in self.steps[start : self.at]]

    def until(self, piece):
        if not self.steps:
            return
        for _, step in self.steps[self.at : self.ends[piece]]:
            step()
        self.at = max(self.at, self.ends[piece])
        self.clock = max(self.clock, self.steps[self.ends[piece] - 1][0])

    def spend(self, micros):
        for step in self.due():
            step()
        self.clock += micros

    def loop(self, count, body, micros):
        turns = []
        for _ in range(count):
            turns.append(self.due())
            self.clock += micros

        @pl.loop(0, count)
        def _(i):
            for turn, mine in enumerate(turns):
                if mine:

                    @pl.when(i == turn)
                    def _():
                        for step in mine:
                            step()

            body(i)


def sum_small(gather, small, small_sem, send_sem):
    me = (gather.x, gather.y, gather.z, gather.c)
    sibling = (gather.x, gather.y, gather.z, 1 - gather.c)

    def send(slot, to, into):
        pltpu.make_async_remote_copy(
            src_ref=small.at[slot],
            dst_ref=small.at[into],
            send_sem=send_sem.at[into],
            recv_sem=small_sem.at[into],
            device_id=gather.device(*to),
            device_id_type=MESH,
        ).start()

    def sent(slot):
        pltpu.make_async_copy(small.at[slot], small.at[slot], send_sem.at[slot]).wait()

    def got(slot):
        pltpu.make_async_copy(small.at[slot], small.at[slot], small_sem.at[slot]).wait()

    def first():
        send(0, sibling, 1)

    def second():
        got(1)
        small[2] = small[0] + small[1]
        send(2, gather.to_x(), 3)

    def third():
        got(3)
        small[4] = small[2] + small[3]
        send(4, gather.to_y(), 5)

    def fourth():
        got(5)
        small[6 + gather.z] = small[4] + small[5]
        for step in (-1, 1):
            gather.onward(step, lambda: send_column(step, gather.z))

    def send_column(step, zs):
        slot = 6 + zs
        pltpu.make_async_remote_copy(
            src_ref=small.at[slot],
            dst_ref=small.at[slot],
            send_sem=send_sem.at[6 + (step + 1) // 2],
            recv_sem=small_sem.at[slot],
            device_id=gather.device(*gather.to_z(step)),
            device_id_type=MESH,
        ).start()

    def pass_on(step, zs):
        got(6 + zs)
        gather.onward(step, lambda: send_far(step, zs))

    def send_far(step, zs):
        slot = 6 + zs
        pltpu.make_async_remote_copy(
            src_ref=small.at[slot],
            dst_ref=small.at[slot],
            send_sem=send_sem.at[8 + slot],
            recv_sem=small_sem.at[slot],
            device_id=gather.device(*gather.to_z(step)),
            device_id_type=MESH,
        ).start()

    def wait_far(step, zs):
        gather.onward(step, lambda: sent_as(6 + zs, 8 + 6 + zs))

    def sent_as(slot, sem):
        pltpu.make_async_copy(small.at[slot], small.at[slot], send_sem.at[sem]).wait()

    def last():
        sent(1), sent(3), sent(5)
        for step in (-1, 1):
            gather.onward(step, lambda: sent_as(6, 6 + (step + 1) // 2))
        for distance in (1, 2, 3):
            for act in gather.both(distance, wait_far):
                act()

    steps = [first, second, third, fourth]
    for distance in (1, 2, 3):
        steps += list(gather.both(distance, pass_on))
    return steps, last


def norm_rows(values, gain, shift):
    center = values - jnp.mean(values, -1, keepdims=True)
    inverse = lax.rsqrt(jnp.mean(center * center, -1, keepdims=True) + 1e-05)
    hat = center * inverse
    return hat * gain + shift, hat, inverse


def norm_back(grad, hat, inverse, gain):
    grad_hat = grad * gain
    return inverse * (
        grad_hat
        - jnp.mean(grad_hat, -1, keepdims=True)
        - hat * jnp.mean(grad_hat * hat, -1, keepdims=True)
    )


def place_adapters(layer, down_ref, up_ref, a16t, b2):
    rank, width = down_ref.shape[2:]
    a16t[...] = jnp.concatenate([down_ref[layer, 0].astype(F32), down_ref[layer, 1].astype(F32)], 0).astype(BF)
    b2[...] = jnp.zeros_like(b2)
    b2[0:16, 0:width] = (2.0 * dot(picker(16, rank, 0), up_ref[layer, 0], 1, 0)).astype(BF)
    b2[0:16, 2 * width : 3 * width] = (
        2.0 * dot(picker(16, rank, rank), up_ref[layer, 1], 1, 0)
    ).astype(BF)


class Exchange:
    def __init__(self, layer, gather, part, half, incoming, sums, send_sem, recv_sem):
        self.layer, self.gather, self.part, self.half = layer, gather, part, half
        self.incoming, self.sums = incoming.at[layer], sums.at[layer]
        self.send_sem, self.recv_sem = send_sem.at[layer], recv_sem.at[layer]
        self.rows = pl.ds(32 * layer, 32)

    def copy(self, source, slot, to):
        return pltpu.make_async_remote_copy(
            src_ref=self.sums.at[source],
            dst_ref=self.incoming.at[slot],
            send_sem=self.send_sem.at[slot],
            recv_sem=self.recv_sem.at[slot],
            device_id=self.gather.device(*to),
            device_id_type=MESH,
        )

    def copies(self, stage):
        g = self.gather
        x, y, z, c = g.x, g.y, g.z, g.c
        if stage == 0:
            return [self.copy(0, 0, g.to_y())]
        if stage == 1:
            places = [(x, y, z, 1 - c), (1 - x, y, z, c), (1 - x, y, z, 1 - c)]
        else:
            places = [(x, y, lax.rem(z + step, 4), c) for step in (1, 2, 3)]
        return [self.copy(stage, 3 * stage - 2 + number, to) for number, to in enumerate(places)]

    def start(self):
        width = self.part.shape[1]
        values = self.part[self.rows]
        left, right = values[:, : width // 2], values[:, width // 2 :]
        first = self.gather.y == 0
        self.half[self.rows] = jnp.where(first, left, right)
        self.sums[0] = jnp.where(first, right, left).astype(BF)
        for copy in self.copies(0):
            copy.start()

    def add(self, stage):
        total = self.half[self.rows]
        for number, copy in enumerate(self.copies(stage)):
            copy.wait_recv()
            total = total + self.incoming[3 * stage - 2 + number if stage else 0].astype(F32)
        return total

    def go_on(self, stage):
        total = self.add(stage)
        self.half[self.rows] = total
        self.sums[stage + 1] = total.astype(BF)
        for copy in self.copies(stage + 1):
            copy.start()

    def finish(self, down, up):
        total = self.add(2)
        down[self.layer] = total[:16]
        up[self.layer] = total[16:]
        for stage in range(3):
            for copy in self.copies(stage):
                copy.wait_send()


def layers_kernel(fast, names_in, names_out, names_scratch, *refs):
    r = types.SimpleNamespace(**dict(zip(names_in + names_out + names_scratch, refs, strict=True)))
    layers = 2
    blocks = r.blocks
    pack_rows, width = r.tokens.shape
    triple, hidden = 3 * width, r.g.shape[1]
    head_dim = width // HEADS
    part_rows = blocks.shape[2]
    per_width = width // part_rows
    pieces = 3 * layers
    x, narrow, rows, probs = r.x, r.narrow, r.rows, r.probs
    inputs = (r.tokens, r.xb)
    slots = probs.shape[0]
    group, ahead = GROUP, slots // GROUP

    if fast:
        gather = Gather(blocks, r.arrive_sem, r.sibling_sem, r.send_sem)
        others = gather.greet()
        me = gather.index(gather.x, gather.y, gather.z, gather.c)
        for layer in range(layers):
            both = jnp.concatenate([r.qkv_w[layer].astype(F32), r.o_w[layer].astype(F32)], 0)
            blocks[3 * layer, me] = both.astype(BF)
        loads = []
        for layer in range(layers):
            for number, source in enumerate((r.up_w, r.down_w)):
                target = blocks.at[3 * layer + 1 + number, me]
                loads.append(pltpu.make_async_copy(source.at[layer], target, r.load_sem.at[len(loads)]))
                loads[-1].start()
        pl.semaphore_wait(pltpu.get_barrier_semaphore(), others)
        for copy in loads:
            copy.wait()
        gather.own(0)
        small = r.small
        own = jnp.zeros((SMALL_ROWS, width), F32)
        few = r.bias.shape[1]
        per_row = width // few
        spot = picker(width, few, lax.rem(me, per_row) * few)
        thin = r.gains.shape[2]
        thin_spot = picker(width, thin, me * thin)
        row = lax.broadcasted_iota(jnp.int32, (SMALL_ROWS, width), 0)
        spread = dot(r.bias[...], spot, 1, 1)
        for layer in range(layers):
            own = jnp.where(row == 8 * layer + me // per_row, spread[layer : layer + 1], own)
            for kind, values in enumerate((r.gains, r.shifts)):
                thin_rows = dot(values[layer], thin_spot, 1, 1)
                for which in range(2):
                    at = 16 + 4 * layer + 2 * kind + which
                    own = jnp.where(row == at, thin_rows[which : which + 1], own)
        small[0] = own.astype(BF)
        small_steps, small_end = sum_small(gather, small, r.small_sem, r.small_send)
        steps, ends = gather.timetable(pieces)
        last_of = [steps[end - 1] for end in ends]
        steps += [(1.5 * number, step) for number, step in enumerate(small_steps)]
        steps.sort(key=lambda entry: entry[0])
        weaver = Weaver(steps, [steps.index(entry) + 1 for entry in last_of])
        exchanges = [
            Exchange(layer, gather, r.part, r.half, r.incoming, r.sums, r.sum_send, r.sum_recv)
            for layer in range(layers)
        ]
    else:
        for number, piece in enumerate((1, 2, 4, 5)):
            pltpu.make_async_copy(r.ud_in.at[number], blocks.at[piece], r.load_sem.at[piece]).start()
        rows[...] = r.small_in[...]
        weaver = Weaver([], [])

    segment = r.segment[...]
    ids = lax.broadcasted_iota(jnp.int32, (16, pack_rows), 0)
    same = ids == segment
    r.one_hot[...] = same.astype(F32).astype(BF)
    r.ones[...] = jnp.ones_like(r.ones)
    r.apart[...] = jnp.where(jnp.logical_or(same, ids >= 4), 0.0, FAR).astype(BF)
    x[...] = r.tokens[...].astype(F32)
    for layer in range(layers):
        place_adapters(layer, r.down, r.up, r.a16t.at[layer], r.b2.at[layer])
        r.ut[layer, 16:32] = (ids == 0).astype(F32).astype(BF)

    def joined(layer, start, count):
        found = blocks[0, pl.ds(start, count)] if fast and layer else r.joined[pl.ds(start, count)]
        return found.reshape(count * part_rows, width)

    def matrix(k, start, count):
        return blocks[k, pl.ds(start, count)].reshape(count * part_rows, width)

    def arrived(k):
        if not fast:
            if k == 3:
                slopes_copy(0, True).wait()
            if k % 3 == 0:
                copy = pltpu.make_async_copy(r.joined_in.at[k // 3], r.joined, r.load_sem.at[k])
                copy.start()
                copy.wait()
            else:
                pltpu.make_async_copy(blocks.at[k], blocks.at[k], r.load_sem.at[k]).wait()
            return
        weaver.until(k)
        gather.from_sibling(k)
        if k % 3:
            return
        target = r.joined if k == 0 else blocks.at[0]
        if k:
            slopes_copy(0, True).wait()
        joint = r.qkv_w.shape[1]
        @pl.loop(0, 8)
        def _(i):
            found = [blocks[k, 4 * i + member].astype(F32) for member in range(4)]
            wide = jnp.concatenate([block[:joint] for block in found], 0).astype(BF)
            target[pl.ds(3 * i, 3)] = wide.reshape(3, part_rows, width)
            target[24 + i] = jnp.concatenate([block[joint:] for block in found], 0).astype(BF)

    def keep_inverse(layer, which, inverse):
        lane = lax.broadcasted_iota(jnp.int32, r.inv.shape, 1)
        r.inv[...] = jnp.where(lane == 2 * layer + which, inverse, r.inv[...])

    def probs_copy(layer, j, slot, out):
        here, there = probs.at[slot], r.probs_out.at[layer, j]
        return pltpu.make_async_copy(here if out else there, there if out else here, r.probs_sem.at[slot])

    whole, spare = divmod(pack_rows, part_rows)
    stride = whole + (1 if spare else 0)
    held = (hidden // width) * stride

    def put_slopes(k, i, values):
        blocks[k, pl.ds(i * stride, whole)] = values[: whole * part_rows].reshape(whole, part_rows, width)
        if spare:
            blocks[k, i * stride + whole, 0:spare] = values[whole * part_rows :]

    def get_slopes(k, i):
        values = blocks[k, pl.ds(i * stride, whole)].reshape(whole * part_rows, width)
        if spare:
            values = jnp.concatenate([values, blocks[k, i * stride + whole, 0:spare]], 0)
        return values

    def slopes_copy(k, out):
        here, there = blocks.at[k, pl.ds(0, held)], r.slopes_out
        return pltpu.make_async_copy(here if out else there, there if out else here, r.slopes_sem)

    for layer in range(layers):
        bias, norm, base = 8 * layer, 16 + 4 * layer, 3 * layer
        qkvt, ot, ut, b2 = r.qkvt.at[layer], r.ot.at[layer], r.ut.at[layer], r.b2.at[layer]
        xb = inputs[layer]
        arrived(base)
        if fast and layer == 0:
            rows[...] = (
                small[6].astype(F32) + small[7].astype(F32) + small[8].astype(F32) + small[9].astype(F32)
            )
        first_row = lax.broadcasted_iota(jnp.int32, (16, width), 0) == 0
        b2[16:32, 0:width] = jnp.where(first_row, rows[bias : bias + 1], 0.0).astype(BF)
        b2[16:32, 2 * width : triple] = jnp.where(first_row, rows[bias + 1 : bias + 2], 0.0).astype(BF)
        ut[0:16] = dot(r.a16t[layer], xb[...], 1, 1).astype(BF)

        for which in range(3):
            weaver.spend(1.0)
            here = slice(which * width, (which + 1) * width)
            found = dot(joined(layer, which * per_width, per_width), xb[...], 1, 1)
            if which != 1:
                found = found + dot(b2[:, here], ut[...], 0, 0)
            found = found.astype(BF)
            qkvt[here] = (found.astype(F32) * head_dim**-0.5).astype(BF) if which == 0 else found

        def attend(i):
            for member in range(group):
                j = i * group + member
                at = pl.multiple_of(j * head_dim, head_dim)
                slot = lax.rem(i, ahead) * group + member
                queries = jnp.concatenate([qkvt[pl.ds(at, head_dim)], r.one_hot[...]], 0)
                keys = jnp.concatenate([qkvt[pl.ds(width + at, head_dim)], r.apart[...]], 0)
                values = jnp.concatenate([qkvt[pl.ds(2 * width + at, head_dim)], r.ones[...]], 0)
                scores = dot(keys, queries, 0, 0)
                weights = jnp.exp(scores - jnp.max(scores, 0, keepdims=True)).astype(BF)
                copy = probs_copy(layer, j, slot, True)
                pl.when(i >= ahead)(copy.wait)
                probs[slot] = weights
                copy.start()
                mixed = dot(values, weights, 1, 0)
                share = 1.0 / mixed[head_dim : head_dim + 1]
                ot[pl.ds(at, head_dim)] = (mixed[:head_dim] * share).astype(BF)
                r.shares[layer, pl.ds(j, 1)] = share

        weaver.loop(HEADS // group, attend, 0.15 + 0.5 * group)
        for slot in range(slots):
            probs_copy(layer, 0, slot, True).wait()

        weaver.spend(1.0)
        values = dot(ot[...].T, joined(layer, 3 * per_width, per_width), 1, 1)
        values = x[...] + (values + rows[bias + 2 : bias + 3])
        normed, hat, inverse = norm_rows(values, rows[norm : norm + 1], rows[norm + 2 : norm + 3])
        x[...] = normed
        narrow[...] = normed.astype(BF)
        r.hat[layer, 0] = hat.astype(BF)
        keep_inverse(layer, 0, inverse)
        weaver.spend(0.5)
        arrived(base + 1)
        def raise_up(i):
            columns = pl.ds(pl.multiple_of(i * width, width), width)
            pre = dot(narrow[...], matrix(base + 1, i * per_width, per_width), 1, 1) + rows[pl.ds(bias + 3 + i, 1)]
            phi = 0.5 * (1.0 + lax.erf(pre * 0.7071067811865476))
            r.g[:, columns] = (pre * phi).astype(BF)
            slope = (phi + pre * 0.3989422804014327 * jnp.exp(-0.5 * pre * pre)).astype(BF)
            put_slopes(base, i, slope)

        if fast:
            gather.drain(base)
        weaver.loop(hidden // width, raise_up, 1.1)
        if layer == 0:
            slopes_copy(0, True).start()
        else:
            grad_copy = pltpu.make_async_copy(r.grad_in, narrow, r.load_grad)
            grad_copy.start()
        arrived(base + 2)
        if layer == 0:
            for at in range(0, width, 256):
                columns = slice(at, at + 256)
                weaver.spend(1.0)
                lowered = dot(r.g[...], blocks[base + 2, :, :, columns].reshape(hidden, 256), 1, 0)
                x[:, columns] += lowered + rows[bias + 7 : bias + 8, columns]
            weaver.spend(0.5)
            values = x[...]
        else:
            lowered = dot(r.g[...], matrix(base + 2, 0, 4 * per_width), 1, 0)
            values = x[...] + (lowered + rows[bias + 7 : bias + 8])
        normed, hat, inverse = norm_rows(values, rows[norm + 1 : norm + 2], rows[norm + 3 : norm + 4])
        r.hat[layer, 1] = hat.astype(BF)
        keep_inverse(layer, 1, inverse)
        if layer == 0:
            x[...] = normed
            r.xb[...] = normed.astype(BF)
        else:
            r.g[:, 0:width] = normed.astype(BF)

    out_copy = pltpu.make_async_copy(r.g.at[:, pl.ds(0, width)], r.block_out, r.out_sem)
    out_copy.start()
    grad_copy.wait()
    x[...] = narrow[...].astype(F32)

    def fetch_first(layer):
        for j in range(slots):
            probs_copy(layer, j, j, False).start()

    def back_norm(layer, which):
        gain = 16 + 4 * layer + which
        inverse = r.inv[:, 2 * layer + which : 2 * layer + which + 1]
        found = norm_back(x[...], r.hat[layer, which].astype(F32), inverse, rows[gain : gain + 1])
        x[...] = found
        narrow[...] = found.astype(BF)

    for layer in reversed(range(layers)):
        base = 3 * layer
        qkvt, ot, b2 = r.qkvt.at[layer], r.ot.at[layer], r.b2.at[layer]
        fetch_first(layer)
        back_norm(layer, 1)
        if layer:
            out_copy.wait()

        if layer == 0:
            slopes_copy(3, False).wait()
        for i in range(hidden // width):
            columns = slice(i * width, (i + 1) * width)
            found = dot(narrow[...], matrix(base + 2, i * per_width, per_width), 1, 1)
            r.g[:, columns] = (found * get_slopes(3, i).astype(F32)).astype(BF)
        if layer:
            slopes_copy(3, False).start()

        if fast and layer == 0:
            exchanges[1].go_on(0)
        x[...] += dot(r.g[...], matrix(base + 1, 0, 4 * per_width), 1, 0)
        back_norm(layer, 0)
        if fast and layer == 0:
            exchanges[1].go_on(1)
        outward = dot(joined(layer, 3 * per_width, per_width), narrow[...], 0, 1)
        for j in range(HEADS):
            here = slice(j * head_dim, (j + 1) * head_dim)
            piece = outward[here] * r.shares[layer, j : j + 1]
            r.totals[j : j + 1] = jnp.sum(piece * ot[here].astype(F32), 0, keepdims=True)
            ot[here] = piece.astype(BF)

        @pl.loop(0, HEADS // slots)
        def _(i):
            for member in range(slots):
                j = i * slots + member
                at = pl.multiple_of(j * head_dim, head_dim)
                slot = member
                queries = qkvt[pl.ds(at, head_dim)]
                keys = qkvt[pl.ds(width + at, head_dim)]
                values = qkvt[pl.ds(2 * width + at, head_dim)]
                outward = ot[pl.ds(at, head_dim)]
                probs_copy(layer, j, slot, False).wait()
                weights = probs[slot]
                gvt = dot(outward, weights, 1, 1)
                grad_weights = dot(values, outward, 0, 0)
                grad_scores = (weights.astype(F32) * (grad_weights - r.totals[pl.ds(j, 1)])).astype(BF)
                gqt = dot(keys, grad_scores, 1, 0) * head_dim**-0.5
                gkt = dot(queries, grad_scores, 1, 1)
                qkvt[pl.ds(at, head_dim)] = gqt.astype(BF)
                qkvt[pl.ds(width + at, head_dim)] = gkt.astype(BF)
                qkvt[pl.ds(2 * width + at, head_dim)] = gvt.astype(BF)

                @pl.when(j + slots < HEADS)
                def _():
                    probs_copy(layer, j + slots, slot, False).start()

        ut = r.ut[layer, 0:16]
        low = (
            dot(b2[0:16, 0:width], qkvt[0:width], 1, 0)
            + dot(b2[0:16, 2 * width : triple], qkvt[2 * width : triple], 1, 0)
        ).astype(BF)
        upper = lax.broadcasted_iota(jnp.int32, (16, width), 0) < 8
        r.part[32 * layer + 16 : 32 * layer + 32] = 2.0 * jnp.where(
            upper, dot(ut, qkvt[0:width], 1, 1), dot(ut, qkvt[2 * width : triple], 1, 1)
        )
        r.part[32 * layer : 32 * layer + 16] = dot(low, inputs[layer][...], 1, 0)
        if fast:
            exchanges[layer].start()
            if layer == 0:
                exchanges[1].finish(r.down_out, r.up_out)
        found = dot(qkvt[0:width], joined(layer, 0, per_width), 0, 0)
        if fast and layer == 0:
            exchanges[0].go_on(0)
        found = found + dot(qkvt[width : triple], joined(layer, per_width, 2 * per_width), 0, 0)
        if fast and layer == 0:
            exchanges[0].go_on(1)
        x[...] += found + dot(low, r.a16t[layer], 0, 0)

    r.g[:, 0:width] = x[...].astype(BF)
    grad_out_copy = pltpu.make_async_copy(r.g.at[:, pl.ds(0, width)], r.grad_out, r.out_sem)
    grad_out_copy.start()
    if fast:
        exchanges[0].finish(r.down_out, r.up_out)
        small_end()
        for k in (1, 2, 4, 5):
            gather.drain(k)
    grad_out_copy.wait()


def hand_over(count, *refs):
    for source, target in zip(refs[:count], refs[count:], strict=True):
        target[...] = source[...]


def vmem_whole():
    return pl.BlockSpec(memory_space=pltpu.VMEM)


def anywhere():
    return pl.BlockSpec(memory_space=pl.ANY)


def shape(dims, kind):
    return jax.ShapeDtypeStruct(dims, kind)


def run_kernel(body, inputs, in_vmem, outputs, out_vmem, scratch, params, cost):
    names_in, names_out, names_scratch = tuple(inputs), tuple(outputs), tuple(scratch)
    found = pl.pallas_call(
        functools.partial(body, names_in, names_out, names_scratch),
        out_shape=[outputs[name] for name in names_out],
        in_specs=[vmem_whole() if name in in_vmem else anywhere() for name in names_in],
        out_specs=[vmem_whole() if name in out_vmem else anywhere() for name in names_out],
        scratch_shapes=[scratch[name] for name in names_scratch],
        compiler_params=params,
        cost_estimate=cost,
    )(*inputs.values())
    return dict(zip(names_out, found, strict=True))


def per_device(
    mesh_sizes,
    tokens,
    segment_index_rows,
    query_key_value_weight,
    attention_output_weight,
    feedforward_up_weight,
    feedforward_down_weight,
    fixed_bias_stack,
    layer_norm_gains,
    layer_norm_shifts,
    adapter_down_factor,
    adapter_up_factor,
    output_gradient,
):
    wide, narrow = mesh_sizes
    devices = wide * narrow
    rows, width = tokens.shape
    layers = query_key_value_weight.shape[0]
    hidden = feedforward_up_weight.shape[2] * devices
    triple = query_key_value_weight.shape[2] * devices
    fast = (wide, narrow) == (16, 2)
    axes = ("wide", "narrow")
    groups, group = 32, hidden // 32

    inputs = dict(
        tokens=tokens,
        segment=segment_index_rows,
        down=jnp.swapaxes(adapter_down_factor, 2, 3),
        up=adapter_up_factor,
    )
    if fast:
        inputs |= dict(
            qkv_w=jnp.swapaxes(query_key_value_weight, 1, 2),
            o_w=jnp.swapaxes(attention_output_weight, 1, 2),
            up_w=jnp.swapaxes(feedforward_up_weight, 1, 2),
            down_w=feedforward_down_weight,
            bias=fixed_bias_stack,
            gains=layer_norm_gains,
            shifts=layer_norm_shifts,
        )
        in_vmem = set(inputs) - {"up_w", "down_w"}
    else:
        qkv = lax.all_gather(query_key_value_weight, axes, axis=2, tiled=True)
        out = lax.all_gather(attention_output_weight, axes, axis=2, tiled=True)
        up = lax.all_gather(feedforward_up_weight, axes, axis=2, tiled=True)
        down = lax.all_gather(feedforward_down_weight, axes, axis=1, tiled=True)
        biases = lax.all_gather(fixed_bias_stack, axes, axis=1, tiled=True)
        gains = lax.all_gather(layer_norm_gains, axes, axis=2, tiled=True)
        shifts = lax.all_gather(layer_norm_shifts, axes, axis=2, tiled=True)
        joined = jnp.concatenate([jnp.swapaxes(qkv, 1, 2), jnp.swapaxes(out, 1, 2)], 1)
        both = jnp.stack([jnp.swapaxes(up, 1, 2), down], 1)
        few = [biases.reshape(layers * 8, width)]
        for layer in range(layers):
            few += [gains[layer], shifts[layer]]
        few += [jnp.zeros((SMALL_ROWS - 12 * layers, width), BF)]
        in_vmem = set(inputs) | {"small_in"}
        inputs |= dict(
            joined_in=joined.reshape(layers, 4 * width // group, group, width),
            ud_in=both.reshape(2 * layers, groups, group, width),
            small_in=jnp.concatenate(few, 0).astype(F32),
        )
    inputs |= dict(grad_in=output_gradient)

    half = width // narrow
    outputs = dict(
        block_out=shape((rows, width), BF),
        grad_out=shape((rows, width), BF),
        probs_out=shape((layers, HEADS, rows, rows), BF),
        slopes_out=shape((hidden // width * -(-rows // group), group, width), BF),
    )
    dma = pltpu.SemaphoreType.DMA
    scratch = dict(
        blocks=pltpu.VMEM((3 * layers, groups, group, width), BF),
        joined=pltpu.VMEM((groups, group, width), BF),
        rows=pltpu.VMEM((SMALL_ROWS, width), F32),
        x=pltpu.VMEM((rows, width), F32),
        xb=pltpu.VMEM((rows, width), BF),
        narrow=pltpu.VMEM((rows, width), BF),
        qkvt=pltpu.VMEM((layers, triple, rows), BF),
        ot=pltpu.VMEM((layers, width, rows), BF),
        shares=pltpu.VMEM((layers, 16, rows), F32),
        totals=pltpu.VMEM((16, rows), F32),
        probs=pltpu.VMEM((4, rows, rows), BF),
        hat=pltpu.VMEM((layers, 2, rows, width), BF),
        inv=pltpu.VMEM((rows, 128), F32),
        g=pltpu.VMEM((rows, hidden), BF),
        ut=pltpu.VMEM((layers, 32, rows), BF),
        a16t=pltpu.VMEM((layers, 16, width), BF),
        b2=pltpu.VMEM((layers, 32, triple), BF),
        one_hot=pltpu.VMEM((16, rows), BF),
        apart=pltpu.VMEM((16, rows), BF),
        ones=pltpu.VMEM((16, rows), BF),
        probs_sem=dma((4,)),
        slopes_sem=dma,
        load_grad=dma,
        out_sem=dma,
    )
    if fast:
        outputs |= dict(
            down_out=shape((layers, 16, half), F32),
            up_out=shape((layers, 16, half), F32),
        )
        out_vmem = {"down_out", "up_out"}
        scratch |= dict(
            part=pltpu.VMEM((32 * layers, width), F32),
            half=pltpu.VMEM((32 * layers, half), F32),
            incoming=pltpu.VMEM((layers, 7, 32, half), BF),
            sums=pltpu.VMEM((layers, 3, 32, half), BF),
            sum_send=dma((layers, 7)),
            sum_recv=dma((layers, 7)),
            small=pltpu.VMEM((10, SMALL_ROWS, width), BF),
            arrive_sem=dma((3 * layers, 9, 4)),
            sibling_sem=dma((3 * layers, 16)),
            send_sem=dma((3 * layers,)),
            small_sem=dma((10,)),
            small_send=dma((18,)),
            load_sem=dma((4,)),
        )
        params = pltpu.CompilerParams(
            collective_id=0, has_side_effects=True, vmem_limit_bytes=VMEM_BYTES
        )
    else:
        outputs |= dict(part=shape((32 * layers, width), F32))
        out_vmem = {"part"}
        scratch |= dict(load_sem=dma((3 * layers,)))
        params = pltpu.CompilerParams(vmem_limit_bytes=VMEM_BYTES)
    products = layers * rows * (width * (triple + width + 2 * hidden) * 2 + 7 * rows * width)
    cost = pl.CostEstimate(flops=2 * products, bytes_accessed=100 << 20, transcendentals=0)
    found = run_kernel(
        functools.partial(layers_kernel, fast), inputs, in_vmem, outputs, out_vmem, scratch, params, cost
    )
    if fast:
        results = [found["block_out"], found["grad_out"], found["down_out"], found["up_out"]]
        results = pl.pallas_call(
            functools.partial(hand_over, 4),
            out_shape=[shape(value.shape, value.dtype) for value in results],
            in_specs=[vmem_whole()] * 4,
            out_specs=[vmem_whole()] * 4,
        )(*results)
    else:
        total = lax.psum_scatter(found["part"].astype(BF), "narrow", scatter_dimension=1, tiled=True)
        total = lax.psum(total, "wide").astype(F32).reshape(layers, 2, 16, half)
        results = [found["block_out"], found["grad_out"], total[:, 0], total[:, 1]]
    block_out, grad_out, down_sum, up_sum = results
    grad_down = jnp.swapaxes(down_sum.reshape(layers, 2, 8, half), 2, 3)
    grad_up = up_sum.reshape(layers, 2, 8, half)
    return (block_out, grad_out, grad_down, grad_up)


def solution(mesh):
    placed = (
        P(("wide", "narrow"), None),
        P(("wide", "narrow"), None),
        P(None, None, ("wide", "narrow")),
        P(None, None, ("wide", "narrow")),
        P(None, None, ("wide", "narrow")),
        P(None, ("wide", "narrow"), None),
        P(None, ("wide", "narrow")),
        P(None, None, ("wide", "narrow")),
        P(None, None, ("wide", "narrow")),
        P(),
        P(),
        P(("wide", "narrow"), None),
    )
    return jax.shard_map(
        functools.partial(per_device, (mesh.shape["wide"], mesh.shape["narrow"])),
        mesh=mesh,
        in_specs=placed,
        out_specs=(
            P(("wide", "narrow"), None),
            P(("wide", "narrow"), None),
            P(None, None, "narrow", None),
            P(None, None, None, "narrow"),
        ),
        check_vma=False,
    )
```

```python
import functools
import types

import jax
import jax.numpy as jnp
from jax import lax
from jax.experimental import pallas as pl
from jax.experimental.pallas import tpu as pltpu
from jax.sharding import PartitionSpec as P

HEADS = 12
BF = jnp.bfloat16
F32 = jnp.float32
MESH = pl.DeviceIdType.MESH
VMEM_BYTES = 63 << 20
SMALL_ROWS = 32
FAR = -(2.0**30)
GROUP = 4
LEAD_US = 2.0
SMALL_US = 2.2
WHEN = tuple(
    tuple(
        16.5 * k + at
        for at in (-12.0, 2.5, 3.0, 0.0, 0.5, 5.0, 5.5, 10.0, 10.5, 6.3, 6.8, 11.5, 12.0, 14.5, 15.0, 7.7, 8.2, 13.0, 13.5, 16.0, 16.5)
        + (18.0, 18.5, 19.5, 20.0, 21.5, 22.0, 17.0)
    )
    for k in range(6)
)


def dot(left, right, left_dim, right_dim):
    return lax.dot_general(
        left, right, (((left_dim,), (right_dim,)), ((), ())), preferred_element_type=F32
    )


def tile16(value):
    return pl.multiple_of(value, 16)


def picker(rows, columns, start):
    down = lax.broadcasted_iota(jnp.int32, (rows, columns), 0)
    across = lax.broadcasted_iota(jnp.int32, (rows, columns), 1)
    return (down == across + start).astype(F32).astype(BF)


class Gather:
    ZC, X, Y, ZE, ZF, XB, XF, YA, YE = range(9)

    def __init__(self, blocks, arrive_sem, sibling_sem, send_sem):
        self.blocks, self.arrive, self.sibling, self.send = blocks, arrive_sem, sibling_sem, send_sem
        wide = lax.axis_index("wide")
        self.y = lax.axis_index("narrow")
        self.c = lax.rem(wide, 2)
        self.x = lax.rem(wide // 2, 2)
        self.z = wide // 4
        self.rows = blocks.shape[2]

    def device(self, x, y, z, c):
        return (z * 4 + x * 2 + c, y)

    def index(self, x, y, z, c):
        return z * 8 + x * 4 + c * 2 + y

    def greet(self):
        entry = pltpu.get_barrier_semaphore()
        x, y, z, c = self.x, self.y, self.z, self.c
        others = [self.to_x(), self.to_y(), (x, y, z, 1 - c), (1 - x, y, z, 1 - c)]
        others += [(x, y, lax.rem(z + step, 4), c) for step in (1, 2, 3)]
        for to in others:
            pl.semaphore_signal(entry, inc=1, device_id=self.device(*to), device_id_type=MESH)
        return len(others)

    def to_x(self):
        return (1 - self.x, self.y, self.z, self.c)

    def to_y(self):
        return (self.x, 1 - self.y, self.z, self.c)

    def to_z(self, step):
        return (self.x, self.y, self.z + step, self.c)

    def onward(self, step, act):
        pl.when(jnp.logical_and(self.z + step >= 0, self.z + step <= 3))(act)

    def part(self, k, source, low, high):
        return self.blocks.at[k, self.index(*source), pl.ds(low, high - low)]

    def push(self, k, source, low, high, to, sem):
        ref = self.part(k, source, low, high)
        pltpu.make_async_remote_copy(
            src_ref=ref,
            dst_ref=ref,
            send_sem=self.send.at[k],
            recv_sem=sem,
            device_id=self.device(*to),
            device_id_type=MESH,
        ).start()

    def got(self, k, source, low, high, sem):
        ref = self.part(k, source, low, high)
        pltpu.make_async_copy(ref, ref, sem).wait()

    def sem(self, k, kind, source_z):
        return self.arrive.at[k, kind, source_z]

    def to_sibling(self, k, source):
        x, y, z, _ = source
        to = (self.x, self.y, self.z, 1 - self.c)
        self.push(k, source, 0, 96, to, self.sibling.at[k, z * 4 + x * 2 + y])

    def own(self, k):
        me = (self.x, self.y, self.z, self.c)
        self.push(k, me, 0, 96, self.to_x(), self.sem(k, self.X, self.z))
        self.push(k, me, 0, 96, self.to_y(), self.sem(k, self.Y, self.z))
        for step in (-1, 1):
            self.onward(
                step,
                lambda: self.push(
                    k, me, 0, 96, self.to_z(step), self.sem(k, self.ZC, self.z)
                ),
            )
        self.to_sibling(k, me)

    def both(self, distance, act):
        for step in (-1, 1):
            source_z = self.z + step * distance
            there = jnp.logical_and(source_z >= 0, source_z <= 3)
            yield functools.partial(pl.when(there), functools.partial(act, -step, source_z))

    def column(self, k, distance):
        def act(step, zs):
            source = (self.x, self.y, zs, self.c)
            self.got(k, source, 0, 96, self.sem(k, self.ZC, zs))
            self.onward(
                step,
                lambda: self.push(k, source, 0, 96, self.to_z(step), self.sem(k, self.ZC, zs)),
            )
            self.push(k, source, 32, 96, self.to_x(), self.sem(k, self.X, zs))
            self.push(k, source, 0, 64, self.to_y(), self.sem(k, self.Y, zs))
            self.to_sibling(k, source)

        return list(self.both(distance, act))

    def direct(self, k):
        def from_x():
            source = (1 - self.x, self.y, self.z, self.c)
            self.got(k, source, 0, 96, self.sem(k, self.X, self.z))
            for step in (-1, 1):
                self.onward(
                    step,
                    lambda: self.push(
                        k, source, 0, 32, self.to_z(step), self.sem(k, self.ZE, self.z)
                    ),
                )
            self.push(k, source, 0, 48, self.to_y(), self.sem(k, self.YA, self.z))
            self.to_sibling(k, source)

        def from_y():
            source = (self.x, 1 - self.y, self.z, self.c)
            self.got(k, source, 0, 96, self.sem(k, self.Y, self.z))
            for step in (-1, 1):
                self.onward(
                    step,
                    lambda: self.push(
                        k, source, 64, 96, self.to_z(step), self.sem(k, self.ZF, self.z)
                    ),
                )
            self.push(k, source, 48, 96, self.to_x(), self.sem(k, self.XB, self.z))
            self.to_sibling(k, source)

        return [from_x, from_y]

    def across(self, k, distance):
        def act(step, zs):
            source = (1 - self.x, self.y, zs, self.c)
            self.got(k, source, 32, 96, self.sem(k, self.X, zs))
            self.push(k, source, 32, 48, self.to_y(), self.sem(k, self.YA, zs))
            source = (self.x, 1 - self.y, zs, self.c)
            self.got(k, source, 0, 64, self.sem(k, self.Y, zs))
            self.push(k, source, 48, 64, self.to_x(), self.sem(k, self.XB, zs))

        return list(self.both(distance, act))

    def along(self, k, distance):
        def act(step, zs):
            source = (1 - self.x, self.y, zs, self.c)
            self.got(k, source, 0, 32, self.sem(k, self.ZE, zs))
            self.onward(
                step,
                lambda: self.push(k, source, 0, 32, self.to_z(step), self.sem(k, self.ZE, zs)),
            )
            self.push(k, source, 0, 32, self.to_y(), self.sem(k, self.YE, zs))
            self.to_sibling(k, source)
            other = (self.x, 1 - self.y, zs, self.c)
            self.got(k, other, 64, 96, self.sem(k, self.ZF, zs))
            self.onward(
                step,
                lambda: self.push(k, other, 64, 96, self.to_z(step), self.sem(k, self.ZF, zs)),
            )
            self.push(k, other, 64, 96, self.to_x(), self.sem(k, self.XF, zs))
            self.to_sibling(k, other)

        return list(self.both(distance, act))

    def corner(self, k, distance):
        def here():
            source = (1 - self.x, 1 - self.y, self.z, self.c)
            self.got(k, source, 48, 96, self.sem(k, self.XB, self.z))
            self.got(k, source, 0, 48, self.sem(k, self.YA, self.z))
            self.to_sibling(k, source)

        def act(step, zs):
            source = (1 - self.x, 1 - self.y, zs, self.c)
            self.got(k, source, 48, 64, self.sem(k, self.XB, zs))
            self.got(k, source, 32, 48, self.sem(k, self.YA, zs))
            self.got(k, source, 64, 96, self.sem(k, self.XF, zs))
            self.got(k, source, 0, 32, self.sem(k, self.YE, zs))
            self.to_sibling(k, source)

        return list(self.both(distance, act)) if distance else [here]

    def timetable(self, pieces):
        order = []
        for k in range(pieces):
            steps = [functools.partial(self.own, k)] + self.direct(k)
            for group in (self.column, self.across, self.along, self.corner):
                for far in (1, 2, 3):
                    steps += group(k, far)
            steps += self.corner(k, 0)
            for at, step in zip(WHEN[k], steps, strict=True):
                if k or step is not steps[0]:
                    order.append((at, len(order), k, step))
        order.sort(key=lambda entry: entry[:2])
        ends = [max(i for i, entry in enumerate(order) if entry[2] == k) + 1 for k in range(pieces)]
        return [(when, step) for when, _, _, step in order], ends

    def from_sibling(self, k):
        @pl.loop(0, 16)
        def _(i):
            source = (lax.rem(i // 2, 2), lax.rem(i, 2), i // 4, 1 - self.c)
            self.got(k, source, 0, 96, self.sibling.at[k, i])

    def drain(self, k):
        def left(blocks, rows):
            ref = self.blocks.at[k, pl.ds(0, blocks), pl.ds(0, rows)]
            pltpu.make_async_copy(ref, ref, self.send.at[k]).wait()

        left(27, 96)
        left(1, 64)

        @pl.when(jnp.logical_and(self.z > 0, self.z < 3))
        def _():
            left(6, 96)
            left(1, 64)


class Weaver:
    def __init__(self, steps, ends):
        self.steps, self.ends = steps, ends
        self.at, self.clock = 0, 0.0

    def due(self):
        start = self.at
        while self.at < len(self.steps) and self.steps[self.at][0] <= self.clock + LEAD_US:
            self.at += 1
        return [step for _, step in self.steps[start : self.at]]

    def until(self, piece):
        if not self.steps:
            return
        for _, step in self.steps[self.at : self.ends[piece]]:
            step()
        self.at = max(self.at, self.ends[piece])
        self.clock = max(self.clock, self.steps[self.ends[piece] - 1][0])

    def spend(self, micros):
        for step in self.due():
            step()
        self.clock += micros

    def loop(self, count, body, micros):
        turns = []
        for _ in range(count):
            turns.append(self.due())
            self.clock += micros

        @pl.loop(0, count)
        def _(i):
            for turn, mine in enumerate(turns):
                if mine:

                    @pl.when(i == turn)
                    def _():
                        for step in mine:
                            step()

            body(i)


def sum_small(gather, small, small_sem, send_sem):
    me = (gather.x, gather.y, gather.z, gather.c)
    sibling = (gather.x, gather.y, gather.z, 1 - gather.c)

    def send(slot, to, into):
        pltpu.make_async_remote_copy(
            src_ref=small.at[slot],
            dst_ref=small.at[into],
            send_sem=send_sem.at[into],
            recv_sem=small_sem.at[into],
            device_id=gather.device(*to),
            device_id_type=MESH,
        ).start()

    def sent(slot):
        pltpu.make_async_copy(small.at[slot], small.at[slot], send_sem.at[slot]).wait()

    def got(slot):
        pltpu.make_async_copy(small.at[slot], small.at[slot], small_sem.at[slot]).wait()

    def first():
        send(0, sibling, 1)

    def second():
        got(1)
        small[2] = small[0] + small[1]
        send(2, gather.to_x(), 3)

    def third():
        got(3)
        small[4] = small[2] + small[3]
        send(4, gather.to_y(), 5)

    def fourth():
        got(5)
        small[6 + gather.z] = small[4] + small[5]
        for step in (-1, 1):
            gather.onward(step, lambda: send_column(step, gather.z))

    def send_column(step, zs):
        slot = 6 + zs
        pltpu.make_async_remote_copy(
            src_ref=small.at[slot],
            dst_ref=small.at[slot],
            send_sem=send_sem.at[6 + (step + 1) // 2],
            recv_sem=small_sem.at[slot],
            device_id=gather.device(*gather.to_z(step)),
            device_id_type=MESH,
        ).start()

    def pass_on(step, zs):
        got(6 + zs)
        gather.onward(step, lambda: send_far(step, zs))

    def send_far(step, zs):
        slot = 6 + zs
        pltpu.make_async_remote_copy(
            src_ref=small.at[slot],
            dst_ref=small.at[slot],
            send_sem=send_sem.at[8 + slot],
            recv_sem=small_sem.at[slot],
            device_id=gather.device(*gather.to_z(step)),
            device_id_type=MESH,
        ).start()

    def wait_far(step, zs):
        gather.onward(step, lambda: sent_as(6 + zs, 8 + 6 + zs))

    def sent_as(slot, sem):
        pltpu.make_async_copy(small.at[slot], small.at[slot], send_sem.at[sem]).wait()

    def last():
        sent(1), sent(3), sent(5)
        for step in (-1, 1):
            gather.onward(step, lambda: sent_as(6, 6 + (step + 1) // 2))
        for distance in (1, 2, 3):
            for act in gather.both(distance, wait_far):
                act()

    steps = [first, second, third, fourth]
    for distance in (1, 2, 3):
        steps += list(gather.both(distance, pass_on))
    return steps, last


def norm_rows(values, gain, shift):
    center = values - jnp.mean(values, -1, keepdims=True)
    inverse = lax.rsqrt(jnp.mean(center * center, -1, keepdims=True) + 1e-05)
    hat = center * inverse
    return hat * gain + shift, hat, inverse


def norm_back(grad, hat, inverse, gain):
    grad_hat = grad * gain
    return inverse * (
        grad_hat
        - jnp.mean(grad_hat, -1, keepdims=True)
        - hat * jnp.mean(grad_hat * hat, -1, keepdims=True)
    )


def place_adapters(layer, down_ref, up_ref, a16t, b2):
    rank, width = down_ref.shape[2:]
    a16t[...] = jnp.concatenate([down_ref[layer, 0].astype(F32), down_ref[layer, 1].astype(F32)], 0).astype(BF)
    b2[...] = jnp.zeros_like(b2)
    b2[0:16, 0:width] = (2.0 * dot(picker(16, rank, 0), up_ref[layer, 0], 1, 0)).astype(BF)
    b2[0:16, 2 * width : 3 * width] = (
        2.0 * dot(picker(16, rank, rank), up_ref[layer, 1], 1, 0)
    ).astype(BF)


class Exchange:
    def __init__(self, layer, gather, part, half, incoming, sums, send_sem, recv_sem):
        self.layer, self.gather, self.part, self.half = layer, gather, part, half
        self.incoming, self.sums = incoming.at[layer], sums.at[layer]
        self.send_sem, self.recv_sem = send_sem.at[layer], recv_sem.at[layer]
        self.rows = pl.ds(32 * layer, 32)

    def copy(self, source, slot, to):
        return pltpu.make_async_remote_copy(
            src_ref=self.sums.at[source],
            dst_ref=self.incoming.at[slot],
            send_sem=self.send_sem.at[slot],
            recv_sem=self.recv_sem.at[slot],
            device_id=self.gather.device(*to),
            device_id_type=MESH,
        )

    def copies(self, stage):
        g = self.gather
        x, y, z, c = g.x, g.y, g.z, g.c
        if stage == 0:
            return [self.copy(0, 0, g.to_y())]
        if stage == 1:
            places = [(x, y, z, 1 - c), (1 - x, y, z, c), (1 - x, y, z, 1 - c)]
        else:
            places = [(x, y, lax.rem(z + step, 4), c) for step in (1, 2, 3)]
        return [self.copy(stage, 3 * stage - 2 + number, to) for number, to in enumerate(places)]

    def start(self):
        width = self.part.shape[1]
        values = self.part[self.rows]
        left, right = values[:, : width // 2], values[:, width // 2 :]
        first = self.gather.y == 0
        self.half[self.rows] = jnp.where(first, left, right)
        self.sums[0] = jnp.where(first, right, left).astype(BF)
        for copy in self.copies(0):
            copy.start()

    def add(self, stage):
        total = self.half[self.rows]
        for number, copy in enumerate(self.copies(stage)):
            copy.wait_recv()
            total = total + self.incoming[3 * stage - 2 + number if stage else 0].astype(F32)
        return total

    def go_on(self, stage):
        total = self.add(stage)
        self.half[self.rows] = total
        self.sums[stage + 1] = total.astype(BF)
        for copy in self.copies(stage + 1):
            copy.start()

    def finish(self, down, up):
        total = self.add(2)
        down[self.layer] = total[:16]
        up[self.layer] = total[16:]
        for stage in range(3):
            for copy in self.copies(stage):
                copy.wait_send()


def layers_kernel(fast, names_in, names_out, names_scratch, *refs):
    r = types.SimpleNamespace(**dict(zip(names_in + names_out + names_scratch, refs, strict=True)))
    layers = 2
    blocks = r.blocks
    pack_rows, width = r.tokens.shape
    triple, hidden = 3 * width, r.g.shape[1]
    head_dim = width // HEADS
    part_rows = blocks.shape[2]
    per_width = width // part_rows
    pieces = 3 * layers
    x, narrow, rows, probs = r.x, r.narrow, r.rows, r.probs
    inputs = (r.tokens, r.xb)
    slots = probs.shape[0]
    group, ahead = GROUP, slots // GROUP

    if fast:
        gather = Gather(blocks, r.arrive_sem, r.sibling_sem, r.send_sem)
        others = gather.greet()
        me = gather.index(gather.x, gather.y, gather.z, gather.c)
        for layer in range(layers):
            both = jnp.concatenate([r.qkv_w[layer].astype(F32), r.o_w[layer].astype(F32)], 0)
            blocks[3 * layer, me] = both.astype(BF)
        loads = []
        for layer in range(layers):
            for number, source in enumerate((r.up_w, r.down_w)):
                target = blocks.at[3 * layer + 1 + number, me]
                loads.append(pltpu.make_async_copy(source.at[layer], target, r.load_sem.at[len(loads)]))
                loads[-1].start()
        pl.semaphore_wait(pltpu.get_barrier_semaphore(), others)
        for copy in loads:
            copy.wait()
        gather.own(0)
        small = r.small
        own = jnp.zeros((SMALL_ROWS, width), F32)
        few = r.bias.shape[1]
        per_row = width // few
        spot = picker(width, few, lax.rem(me, per_row) * few)
        thin = r.gains.shape[2]
        thin_spot = picker(width, thin, me * thin)
        row = lax.broadcasted_iota(jnp.int32, (SMALL_ROWS, width), 0)
        spread = dot(r.bias[...], spot, 1, 1)
        for layer in range(layers):
            own = jnp.where(row == 8 * layer + me // per_row, spread[layer : layer + 1], own)
            for kind, values in enumerate((r.gains, r.shifts)):
                thin_rows = dot(values[layer], thin_spot, 1, 1)
                for which in range(2):
                    at = 16 + 4 * layer + 2 * kind + which
                    own = jnp.where(row == at, thin_rows[which : which + 1], own)
        small[0] = own.astype(BF)
        small_steps, small_end = sum_small(gather, small, r.small_sem, r.small_send)
        steps, ends = gather.timetable(pieces)
        last_of = [steps[end - 1] for end in ends]
        steps += [(SMALL_US * number, step) for number, step in enumerate(small_steps)]
        steps.sort(key=lambda entry: entry[0])
        weaver = Weaver(steps, [steps.index(entry) + 1 for entry in last_of])
        exchanges = [
            Exchange(layer, gather, r.part, r.half, r.incoming, r.sums, r.sum_send, r.sum_recv)
            for layer in range(layers)
        ]
    else:
        for number, piece in enumerate((1, 2, 4, 5)):
            pltpu.make_async_copy(r.ud_in.at[number], blocks.at[piece], r.load_sem.at[piece]).start()
        rows[...] = r.small_in[...]
        weaver = Weaver([], [])

    segment = r.segment[...]
    ids = lax.broadcasted_iota(jnp.int32, (16, pack_rows), 0)
    same = ids == segment
    r.one_hot[...] = same.astype(F32).astype(BF)
    r.ones[...] = jnp.ones_like(r.ones)
    r.apart[...] = jnp.where(jnp.logical_or(same, ids >= 4), 0.0, FAR).astype(BF)
    x[...] = r.tokens[...].astype(F32)
    for layer in range(layers):
        place_adapters(layer, r.down, r.up, r.a16t.at[layer], r.b2.at[layer])
        r.ut[layer, 16:32] = (ids == 0).astype(F32).astype(BF)

    def joined(layer, start, count):
        found = blocks[0, pl.ds(start, count)] if fast and layer else r.joined[pl.ds(start, count)]
        return found.reshape(count * part_rows, width)

    def matrix(k, start, count):
        return blocks[k, pl.ds(start, count)].reshape(count * part_rows, width)

    def arrived(k):
        if not fast:
            if k == 3:
                slopes_copy(0, True).wait()
            if k % 3 == 0:
                copy = pltpu.make_async_copy(r.joined_in.at[k // 3], r.joined, r.load_sem.at[k])
                copy.start()
                copy.wait()
            else:
                pltpu.make_async_copy(blocks.at[k], blocks.at[k], r.load_sem.at[k]).wait()
            return
        weaver.until(k)
        gather.from_sibling(k)
        if k % 3:
            return
        target = r.joined if k == 0 else blocks.at[0]
        if k:
            slopes_copy(0, True).wait()
        joint = r.qkv_w.shape[1]
        @pl.loop(0, 8)
        def _(i):
            found = [blocks[k, 4 * i + member].astype(F32) for member in range(4)]
            wide = jnp.concatenate([block[:joint] for block in found], 0).astype(BF)
            target[pl.ds(3 * i, 3)] = wide.reshape(3, part_rows, width)
            target[24 + i] = jnp.concatenate([block[joint:] for block in found], 0).astype(BF)

    def keep_inverse(layer, which, inverse):
        lane = lax.broadcasted_iota(jnp.int32, r.inv.shape, 1)
        r.inv[...] = jnp.where(lane == 2 * layer + which, inverse, r.inv[...])

    def probs_copy(layer, j, slot, out):
        here, there = probs.at[slot], r.probs_out.at[layer, j]
        return pltpu.make_async_copy(here if out else there, there if out else here, r.probs_sem.at[slot])

    whole, spare = divmod(pack_rows, part_rows)
    stride = whole + (1 if spare else 0)
    held = (hidden // width) * stride

    def put_slopes(k, i, values):
        blocks[k, pl.ds(i * stride, whole)] = values[: whole * part_rows].reshape(whole, part_rows, width)
        if spare:
            blocks[k, i * stride + whole, 0:spare] = values[whole * part_rows :]

    def get_slopes(k, i):
        values = blocks[k, pl.ds(i * stride, whole)].reshape(whole * part_rows, width)
        if spare:
            values = jnp.concatenate([values, blocks[k, i * stride + whole, 0:spare]], 0)
        return values

    def slopes_copy(k, out):
        here, there = blocks.at[k, pl.ds(0, held)], r.slopes_out
        return pltpu.make_async_copy(here if out else there, there if out else here, r.slopes_sem)

    for layer in range(layers):
        bias, norm, base = 8 * layer, 16 + 4 * layer, 3 * layer
        qkvt, ot, ut, b2 = r.qkvt.at[layer], r.ot.at[layer], r.ut.at[layer], r.b2.at[layer]
        xb = inputs[layer]
        arrived(base)
        if fast and layer == 0:
            rows[...] = (
                small[6].astype(F32) + small[7].astype(F32) + small[8].astype(F32) + small[9].astype(F32)
            )
        first_row = lax.broadcasted_iota(jnp.int32, (16, width), 0) == 0
        b2[16:32, 0:width] = jnp.where(first_row, rows[bias : bias + 1], 0.0).astype(BF)
        b2[16:32, 2 * width : triple] = jnp.where(first_row, rows[bias + 1 : bias + 2], 0.0).astype(BF)
        ut[0:16] = dot(r.a16t[layer], xb[...], 1, 1).astype(BF)

        for which in range(3):
            weaver.spend(1.0)
            here = slice(which * width, (which + 1) * width)
            found = dot(joined(layer, which * per_width, per_width), xb[...], 1, 1)
            if which != 1:
                found = found + dot(b2[:, here], ut[...], 0, 0)
            found = found.astype(BF)
            qkvt[here] = (found.astype(F32) * head_dim**-0.5).astype(BF) if which == 0 else found

        def attend(i):
            for member in range(group):
                j = i * group + member
                at = pl.multiple_of(j * head_dim, head_dim)
                slot = lax.rem(i, ahead) * group + member
                queries = jnp.concatenate([qkvt[pl.ds(at, head_dim)], r.one_hot[...]], 0)
                keys = jnp.concatenate([qkvt[pl.ds(width + at, head_dim)], r.apart[...]], 0)
                values = jnp.concatenate([qkvt[pl.ds(2 * width + at, head_dim)], r.ones[...]], 0)
                scores = dot(keys, queries, 0, 0)
                weights = jnp.exp(scores - jnp.max(scores, 0, keepdims=True)).astype(BF)
                copy = probs_copy(layer, j, slot, True)
                pl.when(i >= ahead)(copy.wait)
                probs[slot] = weights
                copy.start()
                mixed = dot(values, weights, 1, 0)
                share = 1.0 / mixed[head_dim : head_dim + 1]
                ot[pl.ds(at, head_dim)] = (mixed[:head_dim] * share).astype(BF)
                r.shares[layer, pl.ds(j, 1)] = share

        weaver.loop(HEADS // group, attend, 0.15 + 0.5 * group)
        for slot in range(slots):
            probs_copy(layer, 0, slot, True).wait()

        weaver.spend(1.0)
        values = dot(ot[...].T, joined(layer, 3 * per_width, per_width), 1, 1)
        values = x[...] + (values + rows[bias + 2 : bias + 3])
        normed, hat, inverse = norm_rows(values, rows[norm : norm + 1], rows[norm + 2 : norm + 3])
        x[...] = normed
        narrow[...] = normed.astype(BF)
        r.hat[layer, 0] = hat.astype(BF)
        keep_inverse(layer, 0, inverse)
        weaver.spend(0.5)
        arrived(base + 1)
        def raise_up(i):
            columns = pl.ds(pl.multiple_of(i * width, width), width)
            pre = dot(narrow[...], matrix(base + 1, i * per_width, per_width), 1, 1) + rows[pl.ds(bias + 3 + i, 1)]
            phi = 0.5 * (1.0 + lax.erf(pre * 0.7071067811865476))
            r.g[:, columns] = (pre * phi).astype(BF)
            slope = (phi + pre * 0.3989422804014327 * jnp.exp(-0.5 * pre * pre)).astype(BF)
            put_slopes(base, i, slope)

        if fast:
            gather.drain(base)
        weaver.loop(hidden // width, raise_up, 1.1)
        if layer == 0:
            slopes_copy(0, True).start()
        else:
            grad_copy = pltpu.make_async_copy(r.grad_in, narrow, r.load_grad)
            grad_copy.start()
        arrived(base + 2)
        if layer == 0:
            for at in range(0, width, 256):
                columns = slice(at, at + 256)
                weaver.spend(1.0)
                lowered = dot(r.g[...], blocks[base + 2, :, :, columns].reshape(hidden, 256), 1, 0)
                x[:, columns] += lowered + rows[bias + 7 : bias + 8, columns]
            weaver.spend(0.5)
            values = x[...]
        else:
            lowered = dot(r.g[...], matrix(base + 2, 0, 4 * per_width), 1, 0)
            values = x[...] + (lowered + rows[bias + 7 : bias + 8])
        normed, hat, inverse = norm_rows(values, rows[norm + 1 : norm + 2], rows[norm + 3 : norm + 4])
        r.hat[layer, 1] = hat.astype(BF)
        keep_inverse(layer, 1, inverse)
        if layer == 0:
            x[...] = normed
            r.xb[...] = normed.astype(BF)
        else:
            r.g[:, 0:width] = normed.astype(BF)

    out_copy = pltpu.make_async_copy(r.g.at[:, pl.ds(0, width)], r.block_out, r.out_sem)
    out_copy.start()
    grad_copy.wait()
    x[...] = narrow[...].astype(F32)

    def fetch_first(layer):
        for j in range(slots):
            probs_copy(layer, j, j, False).start()

    def back_norm(layer, which):
        gain = 16 + 4 * layer + which
        inverse = r.inv[:, 2 * layer + which : 2 * layer + which + 1]
        found = norm_back(x[...], r.hat[layer, which].astype(F32), inverse, rows[gain : gain + 1])
        x[...] = found
        narrow[...] = found.astype(BF)

    for layer in reversed(range(layers)):
        base = 3 * layer
        qkvt, ot, b2 = r.qkvt.at[layer], r.ot.at[layer], r.b2.at[layer]
        fetch_first(layer)
        back_norm(layer, 1)
        if layer:
            out_copy.wait()

        if layer == 0:
            slopes_copy(3, False).wait()
        for i in range(hidden // width):
            columns = slice(i * width, (i + 1) * width)
            found = dot(narrow[...], matrix(base + 2, i * per_width, per_width), 1, 1)
            r.g[:, columns] = (found * get_slopes(3, i).astype(F32)).astype(BF)
        if layer:
            slopes_copy(3, False).start()

        if fast and layer == 0:
            exchanges[1].go_on(0)
        x[...] += dot(r.g[...], matrix(base + 1, 0, 4 * per_width), 1, 0)
        back_norm(layer, 0)
        if fast and layer == 0:
            exchanges[1].go_on(1)
        outward = dot(joined(layer, 3 * per_width, per_width), narrow[...], 0, 1)
        for j in range(HEADS):
            here = slice(j * head_dim, (j + 1) * head_dim)
            piece = outward[here] * r.shares[layer, j : j + 1]
            r.totals[j : j + 1] = jnp.sum(piece * ot[here].astype(F32), 0, keepdims=True)
            ot[here] = piece.astype(BF)

        @pl.loop(0, HEADS // slots)
        def _(i):
            for member in range(slots):
                j = i * slots + member
                at = pl.multiple_of(j * head_dim, head_dim)
                slot = member
                queries = qkvt[pl.ds(at, head_dim)]
                keys = qkvt[pl.ds(width + at, head_dim)]
                values = qkvt[pl.ds(2 * width + at, head_dim)]
                outward = ot[pl.ds(at, head_dim)]
                probs_copy(layer, j, slot, False).wait()
                weights = probs[slot]
                gvt = dot(outward, weights, 1, 1)
                grad_weights = dot(values, outward, 0, 0)
                grad_scores = (weights.astype(F32) * (grad_weights - r.totals[pl.ds(j, 1)])).astype(BF)
                gqt = dot(keys, grad_scores, 1, 0) * head_dim**-0.5
                gkt = dot(queries, grad_scores, 1, 1)
                qkvt[pl.ds(at, head_dim)] = gqt.astype(BF)
                qkvt[pl.ds(width + at, head_dim)] = gkt.astype(BF)
                qkvt[pl.ds(2 * width + at, head_dim)] = gvt.astype(BF)

                @pl.when(j + slots < HEADS)
                def _():
                    probs_copy(layer, j + slots, slot, False).start()

        ut = r.ut[layer, 0:16]
        low = (
            dot(b2[0:16, 0:width], qkvt[0:width], 1, 0)
            + dot(b2[0:16, 2 * width : triple], qkvt[2 * width : triple], 1, 0)
        ).astype(BF)
        upper = lax.broadcasted_iota(jnp.int32, (16, width), 0) < 8
        r.part[32 * layer + 16 : 32 * layer + 32] = 2.0 * jnp.where(
            upper, dot(ut, qkvt[0:width], 1, 1), dot(ut, qkvt[2 * width : triple], 1, 1)
        )
        r.part[32 * layer : 32 * layer + 16] = dot(low, inputs[layer][...], 1, 0)
        if fast:
            exchanges[layer].start()
            if layer == 0:
                exchanges[1].finish(r.down_out, r.up_out)
        found = dot(qkvt[0:width], joined(layer, 0, per_width), 0, 0)
        if fast and layer == 0:
            exchanges[0].go_on(0)
        found = found + dot(qkvt[width : triple], joined(layer, per_width, 2 * per_width), 0, 0)
        if fast and layer == 0:
            exchanges[0].go_on(1)
        x[...] += found + dot(low, r.a16t[layer], 0, 0)

    r.g[:, 0:width] = x[...].astype(BF)
    grad_out_copy = pltpu.make_async_copy(r.g.at[:, pl.ds(0, width)], r.grad_out, r.out_sem)
    grad_out_copy.start()
    if fast:
        exchanges[0].finish(r.down_out, r.up_out)
        small_end()
        for k in (1, 2, 4, 5):
            gather.drain(k)
    grad_out_copy.wait()


def hand_over(count, *refs):
    for source, target in zip(refs[:count], refs[count:], strict=True):
        target[...] = source[...]


def vmem_whole():
    return pl.BlockSpec(memory_space=pltpu.VMEM)


def anywhere():
    return pl.BlockSpec(memory_space=pl.ANY)


def shape(dims, kind):
    return jax.ShapeDtypeStruct(dims, kind)


def run_kernel(body, inputs, in_vmem, outputs, out_vmem, scratch, params, cost):
    names_in, names_out, names_scratch = tuple(inputs), tuple(outputs), tuple(scratch)
    found = pl.pallas_call(
        functools.partial(body, names_in, names_out, names_scratch),
        out_shape=[outputs[name] for name in names_out],
        in_specs=[vmem_whole() if name in in_vmem else anywhere() for name in names_in],
        out_specs=[vmem_whole() if name in out_vmem else anywhere() for name in names_out],
        scratch_shapes=[scratch[name] for name in names_scratch],
        compiler_params=params,
        cost_estimate=cost,
    )(*inputs.values())
    return dict(zip(names_out, found, strict=True))


def per_device(
    mesh_sizes,
    tokens,
    segment_index_rows,
    query_key_value_weight,
    attention_output_weight,
    feedforward_up_weight,
    feedforward_down_weight,
    fixed_bias_stack,
    layer_norm_gains,
    layer_norm_shifts,
    adapter_down_factor,
    adapter_up_factor,
    output_gradient,
):
    wide, narrow = mesh_sizes
    devices = wide * narrow
    rows, width = tokens.shape
    layers = query_key_value_weight.shape[0]
    hidden = feedforward_up_weight.shape[2] * devices
    triple = query_key_value_weight.shape[2] * devices
    fast = (wide, narrow) == (16, 2)
    axes = ("wide", "narrow")
    groups, group = 32, hidden // 32

    inputs = dict(
        tokens=tokens,
        segment=segment_index_rows,
        down=jnp.swapaxes(adapter_down_factor, 2, 3),
        up=adapter_up_factor,
    )
    if fast:
        inputs |= dict(
            qkv_w=jnp.swapaxes(query_key_value_weight, 1, 2),
            o_w=jnp.swapaxes(attention_output_weight, 1, 2),
            up_w=jnp.swapaxes(feedforward_up_weight, 1, 2),
            down_w=feedforward_down_weight,
            bias=fixed_bias_stack,
            gains=layer_norm_gains,
            shifts=layer_norm_shifts,
        )
        in_vmem = set(inputs) - {"up_w", "down_w"}
    else:
        qkv = lax.all_gather(query_key_value_weight, axes, axis=2, tiled=True)
        out = lax.all_gather(attention_output_weight, axes, axis=2, tiled=True)
        up = lax.all_gather(feedforward_up_weight, axes, axis=2, tiled=True)
        down = lax.all_gather(feedforward_down_weight, axes, axis=1, tiled=True)
        biases = lax.all_gather(fixed_bias_stack, axes, axis=1, tiled=True)
        gains = lax.all_gather(layer_norm_gains, axes, axis=2, tiled=True)
        shifts = lax.all_gather(layer_norm_shifts, axes, axis=2, tiled=True)
        joined = jnp.concatenate([jnp.swapaxes(qkv, 1, 2), jnp.swapaxes(out, 1, 2)], 1)
        both = jnp.stack([jnp.swapaxes(up, 1, 2), down], 1)
        few = [biases.reshape(layers * 8, width)]
        for layer in range(layers):
            few += [gains[layer], shifts[layer]]
        few += [jnp.zeros((SMALL_ROWS - 12 * layers, width), BF)]
        in_vmem = set(inputs) | {"small_in"}
        inputs |= dict(
            joined_in=joined.reshape(layers, 4 * width // group, group, width),
            ud_in=both.reshape(2 * layers, groups, group, width),
            small_in=jnp.concatenate(few, 0).astype(F32),
        )
    inputs |= dict(grad_in=output_gradient)

    half = width // narrow
    outputs = dict(
        block_out=shape((rows, width), BF),
        grad_out=shape((rows, width), BF),
        probs_out=shape((layers, HEADS, rows, rows), BF),
        slopes_out=shape((hidden // width * -(-rows // group), group, width), BF),
    )
    dma = pltpu.SemaphoreType.DMA
    scratch = dict(
        blocks=pltpu.VMEM((3 * layers, groups, group, width), BF),
        joined=pltpu.VMEM((groups, group, width), BF),
        rows=pltpu.VMEM((SMALL_ROWS, width), F32),
        x=pltpu.VMEM((rows, width), F32),
        xb=pltpu.VMEM((rows, width), BF),
        narrow=pltpu.VMEM((rows, width), BF),
        qkvt=pltpu.VMEM((layers, triple, rows), BF),
        ot=pltpu.VMEM((layers, width, rows), BF),
        shares=pltpu.VMEM((layers, 16, rows), F32),
        totals=pltpu.VMEM((16, rows), F32),
        probs=pltpu.VMEM((4, rows, rows), BF),
        hat=pltpu.VMEM((layers, 2, rows, width), BF),
        inv=pltpu.VMEM((rows, 128), F32),
        g=pltpu.VMEM((rows, hidden), BF),
        ut=pltpu.VMEM((layers, 32, rows), BF),
        a16t=pltpu.VMEM((layers, 16, width), BF),
        b2=pltpu.VMEM((layers, 32, triple), BF),
        one_hot=pltpu.VMEM((16, rows), BF),
        apart=pltpu.VMEM((16, rows), BF),
        ones=pltpu.VMEM((16, rows), BF),
        probs_sem=dma((4,)),
        slopes_sem=dma,
        load_grad=dma,
        out_sem=dma,
    )
    if fast:
        outputs |= dict(
            down_out=shape((layers, 16, half), F32),
            up_out=shape((layers, 16, half), F32),
        )
        out_vmem = {"down_out", "up_out"}
        scratch |= dict(
            part=pltpu.VMEM((32 * layers, width), F32),
            half=pltpu.VMEM((32 * layers, half), F32),
            incoming=pltpu.VMEM((layers, 7, 32, half), BF),
            sums=pltpu.VMEM((layers, 3, 32, half), BF),
            sum_send=dma((layers, 7)),
            sum_recv=dma((layers, 7)),
            small=pltpu.VMEM((10, SMALL_ROWS, width), BF),
            arrive_sem=dma((3 * layers, 9, 4)),
            sibling_sem=dma((3 * layers, 16)),
            send_sem=dma((3 * layers,)),
            small_sem=dma((10,)),
            small_send=dma((18,)),
            load_sem=dma((4,)),
        )
        params = pltpu.CompilerParams(
            collective_id=0, has_side_effects=True, vmem_limit_bytes=VMEM_BYTES
        )
    else:
        outputs |= dict(part=shape((32 * layers, width), F32))
        out_vmem = {"part"}
        scratch |= dict(load_sem=dma((3 * layers,)))
        params = pltpu.CompilerParams(vmem_limit_bytes=VMEM_BYTES)
    products = layers * rows * (width * (triple + width + 2 * hidden) * 2 + 7 * rows * width)
    cost = pl.CostEstimate(flops=2 * products, bytes_accessed=100 << 20, transcendentals=0)
    found = run_kernel(
        functools.partial(layers_kernel, fast), inputs, in_vmem, outputs, out_vmem, scratch, params, cost
    )
    if fast:
        results = [found["block_out"], found["grad_out"], found["down_out"], found["up_out"]]
        results = pl.pallas_call(
            functools.partial(hand_over, 4),
            out_shape=[shape(value.shape, value.dtype) for value in results],
            in_specs=[vmem_whole()] * 4,
            out_specs=[vmem_whole()] * 4,
        )(*results)
    else:
        total = lax.psum_scatter(found["part"].astype(BF), "narrow", scatter_dimension=1, tiled=True)
        total = lax.psum(total, "wide").astype(F32).reshape(layers, 2, 16, half)
        results = [found["block_out"], found["grad_out"], total[:, 0], total[:, 1]]
    block_out, grad_out, down_sum, up_sum = results
    grad_down = jnp.swapaxes(down_sum.reshape(layers, 2, 8, half), 2, 3)
    grad_up = up_sum.reshape(layers, 2, 8, half)
    return (block_out, grad_out, grad_down, grad_up)


def solution(mesh):
    placed = (
        P(("wide", "narrow"), None),
        P(("wide", "narrow"), None),
        P(None, None, ("wide", "narrow")),
        P(None, None, ("wide", "narrow")),
        P(None, None, ("wide", "narrow")),
        P(None, ("wide", "narrow"), None),
        P(None, ("wide", "narrow")),
        P(None, None, ("wide", "narrow")),
        P(None, None, ("wide", "narrow")),
        P(),
        P(),
        P(("wide", "narrow"), None),
    )
    return jax.shard_map(
        functools.partial(per_device, (mesh.shape["wide"], mesh.shape["narrow"])),
        mesh=mesh,
        in_specs=placed,
        out_specs=(
            P(("wide", "narrow"), None),
            P(("wide", "narrow"), None),
            P(None, None, "narrow", None),
            P(None, None, None, "narrow"),
        ),
        check_vma=False,
    )
```
